32 devices in a mesh: clu: 4 (over z), ang: 8 (over y, x, core).
Axes of the slice: x: 2, y: 2, z: 4, core: 2. Of those that a mesh axis runs over, the one named last changes fastest.
Arguments:
- patterns7: bfloat16 [8192, 2, 64, 128], P(('clu', 'ang')), may hold values from -6 to 6
- polar_up7: bfloat16 [128, 64], replicated, may hold values from -0.25 to 0.25
- azimuth_up7: bfloat16 [128, 256], replicated, may hold values from -0.5 to 0.5
- polar_up6: bfloat16 [256, 128], replicated, may hold values from -0.1875 to 0.1875
- azimuth_up6: bfloat16 [256, 512], replicated, may hold values from -0.375 to 0.375
- polar_first: int32 [512], replicated, may hold values from 0 to 252, as said below
- polar_weights: bfloat16 [512, 4], replicated, may hold values from -1 to 1
- azimuth_first: int32 [1024], replicated, may hold values from 0 to 511, as said below
- azimuth_weights: bfloat16 [1024, 4], replicated, may hold values from -3 to 3
- transfer5: bfloat16 [316, 2, 256, 512], P(None, None, 'ang', 'clu'), may hold values from -1.5 to 1.5
- sources5: int32 [128, 16], replicated, may hold values from -1 to 127, as said below
- offsets5: int32 [128, 16], replicated, may hold values from -1 to 315, as said below
- transfer4: bfloat16 [316, 2, 512, 1024], P(None, None, 'ang', 'clu'), may hold values from -1.5 to 1.5
- sources4: int32 [16, 16], replicated, may hold values from -1 to 15, as said below
- offsets4: int32 [16, 16], replicated, may hold values from -1 to 315, as said below
Outputs:
- translated5: bfloat16 [128, 2, 256, 512], P(None, None, 'ang', 'clu')
- translated4: bfloat16 [16, 2, 512, 1024], P(None, None, 'ang', 'clu')
The draws below stay inside these ranges and needn't reach their ends.
Inputs may be any that keep to these rules, and one draw needn't show every extreme that they name: The theta stencil of target row r reads source rows polar_first[r] to polar_first[r] + 3, all within floor(r / 2) - 3 to floor(r / 2) + 3. The phi stencil of target column c reads source columns (azimuth_first[c] + k) mod 512, k = 0 to 3, all within floor(c / 2) - 3 to floor(c / 2) + 3 modulo 512. `sources5`: row t lists source clusters of target t: live entries first, then -1; never t itself; at least one live entry. `offsets5`: displacement id of each slot; -1 exactly where sources5 is -1. `sources4`: row t lists source clusters of target t: live entries first, then -1; never t itself; at least one live entry. `offsets4`: displacement id of each slot; -1 exactly where sources4 is -1.
All inputs are finite; a program needn't handle non-finite values.
Results may differ from the reference program's by a relative error of at most 0.015.
Values may be sent and summed in bfloat16 or wider, within the bound.
A program may use at most 192 MiB of HBM per device.

```python
import math
import jax
import jax.numpy as jnp
from jax import lax

T4 = 512
F4 = 1024
LIST = 16
DISP = 316
T5 = 256
F5 = 512
T6 = 128
F6 = 256
T7 = 64
F7 = 128
NC7 = 8192
NC5 = 128
NC4 = 16


def draw_polar_first(key, part):
    target_rows = jnp.arange(T4, dtype=jnp.int32)
    jitter = jax.random.randint(key, (T4,), 0, 2, dtype=jnp.int32)
    return jnp.clip(target_rows // 2 - 1 + jitter, 0, T5 - 4)


def draw_azimuth_first(key, part):
    target_cols = jnp.arange(F4, dtype=jnp.int32)
    jitter = jax.random.randint(key, (F4,), 0, 2, dtype=jnp.int32)
    jitter = jnp.where(target_cols < 4, 0, jitter)
    return (target_cols // 2 - 1 + jitter) % F5


def interaction_lists(key, salt, targets):
    base_key = jax.random.fold_in(key, salt)
    key_source, key_offset, key_count = jax.random.split(base_key, 3)
    target_index = jnp.arange(targets, dtype=jnp.int32)[:, None]
    steps_away = jax.random.randint(key_source, (targets, LIST), 1, targets, dtype=jnp.int32)
    source_ids = (target_index + steps_away) % targets
    offset_ids = jax.random.randint(key_offset, (targets, LIST), 0, DISP, dtype=jnp.int32)
    live_count = jax.random.randint(key_count, (targets,), LIST // 2, LIST + 1, dtype=jnp.int32)
    live_count = live_count.at[0].set(LIST).at[1].set(LIST // 2)
    source_ids = source_ids.at[0, 0].set(targets - 1).at[1, 0].set(0)
    offset_ids = offset_ids.at[0, 0].set(DISP - 1).at[0, 1].set(0)
    live_mask = jnp.arange(LIST, dtype=jnp.int32)[None, :] < live_count[:, None]
    return (jnp.where(live_mask, source_ids, -1), jnp.where(live_mask, offset_ids, -1))


def draw_sources5(key, part):
    return interaction_lists(key, 5, NC5)[0]


def draw_offsets5(key, part):
    return interaction_lists(key, 5, NC5)[1]


def draw_sources4(key, part):
    return interaction_lists(key, 4, NC4)[0]


def draw_offsets4(key, part):
    return interaction_lists(key, 4, NC4)[1]


def block_levels(stream_key, shape, pieces, smallest, top_value):
    level = 1.0
    for axis_at, blocks in pieces:
        steps = jax.random.uniform(jax.random.fold_in(jax.random.fold_in(stream_key, 6), axis_at), (blocks,), jnp.float32, smallest / len(pieces), top_value / len(pieces))
        level = level * jnp.repeat(jnp.exp(steps), shape[axis_at] // blocks).reshape((-1,) + (1,) * (len(shape) - 1 - axis_at))
    return level


def bell_draw(stream_key, dims, spread, most, cuts=(), held_as=jnp.bfloat16):
    array = jax.random.normal(stream_key, dims, jnp.float32) * spread
    if len(cuts) > 0:
        array = block_levels(stream_key, dims, cuts, -0.22, 0.18) * array
    return jnp.clip(array, min=-most, max=most).astype(held_as)


def setup_inputs(seed: int = 0) -> dict:
    seeds = jax.random.split(jax.random.key(seed), 16)
    return {
        "patterns7": bell_draw(seeds[0], (NC7, 2, T7, F7), 1.0, 6.0, ((0, 32),)),
        "polar_up7": bell_draw(seeds[1], (T6, T7), (8 * T7) ** -0.5, 0.25),
        "azimuth_up7": bell_draw(seeds[2], (F7, F6), F7 ** -0.5, 0.5),
        "polar_up6": bell_draw(seeds[3], (T5, T6), (8 * T6) ** -0.5, 0.1875),
        "azimuth_up6": bell_draw(seeds[4], (F6, F5), F6 ** -0.5, 0.375),
        "polar_first": draw_polar_first(jax.random.fold_in(seeds[15], 71), 0),
        "polar_weights": bell_draw(seeds[6], (T4, 4), 32 ** -0.5, 1.0),
        "azimuth_first": draw_azimuth_first(jax.random.fold_in(seeds[15], 71), 0),
        "azimuth_weights": bell_draw(seeds[8], (F4, 4), 4 ** -0.5, 3.0),
        "transfer5": bell_draw(seeds[9], (DISP, 2, T5, F5), 0.25, 1.5, ((2, 8), (3, 4))),
        "sources5": draw_sources5(jax.random.fold_in(seeds[15], 71), 0),
        "offsets5": draw_offsets5(jax.random.fold_in(seeds[15], 71), 0),
        "transfer4": bell_draw(seeds[12], (DISP, 2, T4, F4), 0.25, 1.5, ((2, 8), (3, 4))),
        "sources4": draw_sources4(jax.random.fold_in(seeds[15], 71), 0),
        "offsets4": draw_offsets4(jax.random.fold_in(seeds[15], 71), 0),
    }


def octant_signs():
    octant = jnp.arange(8, dtype=jnp.int32)
    sign_first = (2 * (octant % 2) - 1).astype(jnp.float32)
    sign_second = (2 * ((octant // 2) % 2) - 1).astype(jnp.float32)
    sign_third = (2 * (octant // 4) - 1).astype(jnp.float32)
    return sign_first, sign_second, sign_third


def phase_tables(polar_index, azimuth_index, polar_count, azimuth_count):
    polar_angle = (polar_index + 0.5) * (math.pi / polar_count)
    azimuth_angle = azimuth_index * (2.0 * math.pi / azimuth_count)
    direction_x = jnp.sin(polar_angle)[:, None] * jnp.cos(azimuth_angle)[None, :]
    direction_y = jnp.sin(polar_angle)[:, None] * jnp.sin(azimuth_angle)[None, :]
    direction_z = jnp.cos(polar_angle)[:, None] * jnp.ones_like(azimuth_angle)[None, :]
    sign_first, sign_second, sign_third = octant_signs()
    phase_angle = (polar_count / 8.0) * (sign_first[:, None, None] * direction_x + sign_second[:, None, None] * direction_y + sign_third[:, None, None] * direction_z)
    return jnp.cos(phase_angle), jnp.sin(phase_angle)


def shift_sum(child_terms, cosine, sine):
    real_part = jnp.sum(child_terms[:, :, 0] * cosine - child_terms[:, :, 1] * sine, axis=1)
    imag_part = jnp.sum(child_terms[:, :, 0] * sine + child_terms[:, :, 1] * cosine, axis=1)
    return jnp.stack([real_part, imag_part], axis=1).astype(jnp.bfloat16)


def stencil_matrix(tap_index, weights, column_count):
    matches = (tap_index[:, :, None] == jnp.arange(column_count, dtype=jnp.int32)[None, None, :]).astype(jnp.float32)
    return jnp.sum(weights.astype(jnp.float32)[:, :, None] * matches, axis=1)


def parent_block(children, polar_matrix, azimuth_matrix, cosine, sine):
    parents = children.shape[0] // 8
    grouped = children.reshape(parents, 8, 2, children.shape[2], children.shape[3]).astype(jnp.float32)
    halfway = jnp.einsum("ut,pkcts->pkcus", polar_matrix.astype(jnp.float32), grouped).astype(jnp.bfloat16)
    halfway = lax.optimization_barrier(halfway).astype(jnp.float32)
    child_terms = jnp.einsum("pkcus,sv->pkcuv", halfway, azimuth_matrix.astype(jnp.float32))
    return shift_sum(child_terms, cosine, sine)


def aggregate(children, polar_matrix, azimuth_matrix, cosine, sine, block_parents):
    parent_total = children.shape[0] // 8
    group_size = math.gcd(parent_total, block_parents)
    blocks = children.reshape(parent_total // group_size, group_size * 8, 2, children.shape[2], children.shape[3])

    def one_block(block_piece):
        return parent_block(block_piece, polar_matrix, azimuth_matrix, cosine, sine)

    merged = lax.map(one_block, blocks)
    return merged.reshape(parent_total, 2, polar_matrix.shape[0], azimuth_matrix.shape[1])


def translate(patterns, transfer_table, sources, displacements, block_targets):
    targets = patterns.shape[0]
    group_size = math.gcd(targets, block_targets)
    flat_patterns = patterns.reshape(targets, 2, -1)
    flat_table = transfer_table.reshape(transfer_table.shape[0], 2, -1)

    def one_block(pair):
        source_block, offset_block = pair
        live_mask = (source_block >= 0).astype(jnp.float32)[:, :, None]
        picked = jnp.take(flat_patterns, jnp.maximum(source_block, 0), axis=0).astype(jnp.float32)
        factor = jnp.take(flat_table, jnp.maximum(offset_block, 0), axis=0).astype(jnp.float32)
        real_part = jnp.sum(live_mask * (factor[:, :, 0] * picked[:, :, 0] - factor[:, :, 1] * picked[:, :, 1]), axis=1)
        imag_part = jnp.sum(live_mask * (factor[:, :, 0] * picked[:, :, 1] + factor[:, :, 1] * picked[:, :, 0]), axis=1)
        return jnp.stack([real_part, imag_part], axis=1).astype(jnp.bfloat16)

    slots = sources.shape[1]
    merged = lax.map(one_block, (sources.reshape(targets // group_size, group_size, slots), displacements.reshape(targets // group_size, group_size, slots)))
    return merged.reshape(patterns.shape)


def reference(patterns7, polar_up7, azimuth_up7, polar_up6, azimuth_up6, polar_first, polar_weights, azimuth_first, azimuth_weights, transfer5, sources5, offsets5, transfer4, sources4, offsets4):
    cosine6, sine6 = phase_tables(jnp.arange(T6, dtype=jnp.float32), jnp.arange(F6, dtype=jnp.float32), T6, F6)
    level6 = aggregate(patterns7, polar_up7, azimuth_up7, cosine6, sine6, 64)
    cosine5, sine5 = phase_tables(jnp.arange(T5, dtype=jnp.float32), jnp.arange(F5, dtype=jnp.float32), T5, F5)
    level5 = aggregate(level6, polar_up6, azimuth_up6, cosine5, sine5, 8)
    translated5 = translate(level5, transfer5, sources5, offsets5, 4)
    four_taps = jnp.arange(4, dtype=jnp.int32)[None, :]
    polar_matrix = stencil_matrix(polar_first[:, None] + four_taps, polar_weights, T5)
    azimuth_matrix = stencil_matrix((azimuth_first[:, None] + four_taps) % F5, azimuth_weights, F5).T
    cosine4, sine4 = phase_tables(jnp.arange(T4, dtype=jnp.float32), jnp.arange(F4, dtype=jnp.float32), T4, F4)
    level4 = aggregate(level5, polar_matrix, azimuth_matrix, cosine4, sine4, 2)
    translated4 = translate(level4, transfer4, sources4, offsets4, 1)
    return translated5, translated4
```

```python
import math

import jax
import jax.numpy as jnp
import numpy as np
from jax import lax
from jax.experimental import pallas as pl
from jax.experimental.pallas import tpu as pltpu
from jax.sharding import PartitionSpec as P

VMEM_LIMIT = 58 * 1024 * 1024


def sample_angles(rows, cols):
    polar = (np.arange(rows) + 0.5) * (np.pi / rows)
    azimuth = np.arange(cols) * (2.0 * np.pi / cols)
    return polar, azimuth


def transverse_factors(rows, cols):
    polar, azimuth = sample_angles(rows, cols)
    first = rows / 8.0 * np.sin(polar)[:, None] * np.cos(azimuth)[None, :]
    second = rows / 8.0 * np.sin(polar)[:, None] * np.sin(azimuth)[None, :]
    return np.stack(
        [
            np.cos(first) * np.cos(second),
            np.sin(first) * np.cos(second),
            np.cos(first) * np.sin(second),
            np.sin(first) * np.sin(second),
        ]
    ).astype(np.float32)


def polar_operator(matrix, signs, chunk):
    rows, taps = matrix.shape
    polar, _ = sample_angles(rows, 1)
    axial = rows / 8.0 * np.cos(polar)
    in_phase = matrix.astype(jnp.float32) * np.cos(axial).astype(np.float32)[:, None]
    quadrature = matrix.astype(jnp.float32) * np.sin(axial).astype(np.float32)[:, None]
    real_row = []
    imag_row = []
    for sign in signs:
        real_row += [in_phase, -sign * quadrature]
        imag_row += [sign * quadrature, in_phase]
    whole = jnp.stack([jnp.concatenate(real_row, axis=1), jnp.concatenate(imag_row, axis=1)])
    whole = whole.reshape(2, rows // chunk, chunk, 2 * len(signs) * taps)
    whole = whole.transpose(1, 0, 2, 3)
    return whole.reshape(rows // chunk, 2 * chunk, -1).astype(jnp.bfloat16)


def aggregate_kernel(pairs, width, split, plain, x_ref, m_ref, b_ref, t_ref, *outs):
    parents = x_ref.shape[0]
    rows2, cols = x_ref.shape[3] * x_ref.shape[4], x_ref.shape[5]
    chunk = t_ref.shape[1]
    steps = b_ref.shape[1] // width
    out_plain = outs[0] if plain else None
    out_split = outs[-1] if split else None

    def one_parent(p):
        operator = m_ref[0, 0]
        halves = []
        for child in range(4):
            stacked = [x_ref[p, s, child].reshape(rows2, cols) for s in range(pairs)]
            stacked = stacked[0] if pairs == 1 else jnp.concatenate(stacked, axis=0)
            halves.append(stacked)
        joined = jnp.concatenate(halves, axis=1)
        h = jnp.dot(operator, joined, preferred_element_type=jnp.float32)
        h0, h1, h2, h3 = [h[:, k * cols : (k + 1) * cols] for k in range(4)]
        low_sum, low_diff = h0 + h1, h1 - h0
        high_sum, high_diff = h2 + h3, h3 - h2
        sums = jnp.concatenate(
            [
                (low_sum + high_sum).astype(jnp.bfloat16),
                (low_diff + high_diff).astype(jnp.bfloat16),
                (high_sum - low_sum).astype(jnp.bfloat16),
                (high_diff - low_diff).astype(jnp.bfloat16),
            ],
            axis=0,
        )

        def columns(j, start):
            cut = pl.ds(start, width)
            y = jnp.dot(sums, b_ref[:, cut], preferred_element_type=jnp.float32)
            part = [y[k * chunk : (k + 1) * chunk] for k in range(8)]
            f0, f1, f2, f3 = [t_ref[k, :, cut] for k in range(4)]
            real = f0 * part[0] - f1 * part[3] - f2 * part[5] - f3 * part[6]
            imag = f0 * part[1] + f1 * part[2] + f2 * part[4] - f3 * part[7]
            both = (real.astype(jnp.bfloat16), imag.astype(jnp.bfloat16))
            for c in range(2):
                if plain:
                    out_plain[p, c, :, cut] = both[c]
                if split:
                    band_rows, block_cols = out_split.shape[4], out_split.shape[5]
                    for q in range(width // block_cols):
                        for band in range(chunk // band_rows):
                            out_split[j * (width // block_cols) + q, band, p, c] = both[c][
                                band * band_rows : (band + 1) * band_rows,
                                q * block_cols : (q + 1) * block_cols,
                            ]

        if steps == 1:
            columns(0, 0)
        else:

            @pl.loop(0, steps)
            def _(j):
                columns(j, pl.multiple_of(j * width, width))

    if parents == 1:
        one_parent(0)
    else:

        @pl.loop(0, parents, unroll=2)
        def _(p):
            one_parent(p)


def aggregate(children, operator, azimuth, factors, group, plain, split, name):
    parents, pairs, _, _, taps, cols = children.shape
    per_parent, chunks, chunk2, depth = operator.shape
    chunk = chunk2 // 2
    rows, out_cols = factors.shape[1], factors.shape[2]
    width = min(256, out_cols)
    out_shape = []
    out_specs = []
    if plain:
        out_shape.append(jax.ShapeDtypeStruct((parents, 2, rows, out_cols), jnp.bfloat16))
        out_specs.append(pl.BlockSpec((group, 2, chunk, out_cols), lambda p, u: (p, 0, u, 0)))
    if split is not None:
        blocks, bands = split
        band_rows, block_cols = rows // bands, out_cols // blocks
        width = max(width, block_cols)
        out_shape.append(
            jax.ShapeDtypeStruct(
                (blocks, bands, parents, 2, band_rows, block_cols), jnp.bfloat16
            )
        )
        out_specs.append(
            pl.BlockSpec(
                (blocks, chunk // band_rows, group, 2, band_rows, block_cols),
                lambda p, u: (0, u, p, 0, 0, 0),
            )
        )

    def body(*refs):
        aggregate_kernel(pairs, width, split is not None, plain, *refs)

    if per_parent > 1:
        operator_map = lambda p, u: (p, u, 0, 0)
    else:
        operator_map = lambda p, u: (0, u, 0, 0)
    flops = 2 * parents * chunks * 4 * (chunk2 * depth * cols + chunk2 * cols * out_cols)
    moved = 2 * (children.size + parents * 2 * rows * out_cols) + 4 * factors.size
    return pl.pallas_call(
        body,
        grid=(parents // group, chunks),
        in_specs=[
            pl.BlockSpec((group, pairs, 4, 2, taps, cols), lambda p, u: (p, 0, 0, 0, 0, 0)),
            pl.BlockSpec((1, 1, chunk2, depth), operator_map),
            pl.BlockSpec(azimuth.shape, lambda p, u: (0, 0)),
            pl.BlockSpec((4, chunk, out_cols), lambda p, u: (0, u, 0)),
        ],
        out_specs=out_specs,
        out_shape=out_shape,
        compiler_params=pltpu.CompilerParams(vmem_limit_bytes=VMEM_LIMIT),
        cost_estimate=pl.CostEstimate(flops=flops, bytes_accessed=moved, transcendentals=0),
        name=name,
    )(children, operator, azimuth, factors)


def translate_kernel(slots, merge, src, off, cnt, x_ref, t_ref, o_ref, held):
    targets = o_ref.shape[0]
    sources = held.shape[0] - 1
    held[sources] = jnp.zeros(held.shape[1:], held.dtype)

    @pl.loop(0, sources, unroll=4)
    def _(s):
        if merge == 1:
            held[s] = x_ref[s]
        else:
            total = x_ref[s * merge].astype(jnp.float32)
            for k in range(1, merge):
                total = total + x_ref[s * merge + k].astype(jnp.float32)
            held[s] = total.astype(held.dtype)

    def gather(t, live):
        real = imag = None
        for first in range(0, live, 4):
            group_real = group_imag = None
            for j in range(first, min(first + 4, live)):
                picked = src[t * slots + j]
                chosen = off[t * slots + j]
                pr, pi = held[picked, 0], held[picked, 1]
                fr, fi = t_ref[chosen, 0], t_ref[chosen, 1]
                term_real = fr * pr - fi * pi
                term_imag = fr * pi + fi * pr
                group_real = term_real if group_real is None else group_real + term_real
                group_imag = term_imag if group_imag is None else group_imag + term_imag
            group_real = group_real.astype(jnp.float32)
            group_imag = group_imag.astype(jnp.float32)
            real = group_real if real is None else real + group_real
            imag = group_imag if imag is None else imag + group_imag
        o_ref[t, 0] = real.astype(o_ref.dtype)
        o_ref[t, 1] = imag.astype(o_ref.dtype)

    ends = sorted({min(slots, -(-slots * k // 16) * 4) for k in (2, 3)} | {slots})

    @pl.loop(0, targets)
    def _(t):
        live = cnt[t]
        lower = -1
        for end in ends:

            @pl.when(jnp.logical_and(live > lower, live <= end))
            def _(end=end):
                gather(t, end)

            lower = end


def translate(patterns, table, sources, displacements, row_chunk, merge, name):
    targets, slots = sources.shape
    displacement_count, _, rows, cols = table.shape
    incoming = patterns.shape[0]
    held_count = incoming // merge
    live = sources >= 0
    src = jnp.where(live, sources, held_count).reshape(-1)
    off = jnp.maximum(displacements, 0).reshape(-1)
    cnt = jnp.sum(live.astype(jnp.int32), axis=1)

    def body(*refs):
        translate_kernel(slots, merge, *refs)

    return pl.pallas_call(
        body,
        grid_spec=pltpu.PrefetchScalarGridSpec(
            num_scalar_prefetch=3,
            grid=(rows // row_chunk,),
            in_specs=[
                pl.BlockSpec((incoming, 2, row_chunk, cols), lambda r, *_: (0, 0, r, 0)),
                pl.BlockSpec((displacement_count, 2, row_chunk, cols), lambda r, *_: (0, 0, r, 0)),
            ],
            out_specs=pl.BlockSpec((targets, 2, row_chunk, cols), lambda r, *_: (0, 0, r, 0)),
            scratch_shapes=[pltpu.VMEM((held_count + 1, 2, row_chunk, cols), jnp.bfloat16)],
        ),
        out_shape=jax.ShapeDtypeStruct((targets, 2, rows, cols), jnp.bfloat16),
        compiler_params=pltpu.CompilerParams(vmem_limit_bytes=VMEM_LIMIT),
        cost_estimate=pl.CostEstimate(
            flops=8 * targets * slots * rows * cols,
            bytes_accessed=2 * (patterns.size + table.size),
            transcendentals=0,
        ),
        name=name,
    )(src, off, cnt, patterns, table)


def stencil_matrix(tap_index, weights, column_count):
    matches = (
        tap_index[:, :, None] == jnp.arange(column_count, dtype=jnp.int32)[None, None, :]
    ).astype(jnp.float32)
    return jnp.sum(weights.astype(jnp.float32)[:, :, None] * matches, axis=1)


def shards(
    patterns7,
    polar_up7,
    azimuth_up7,
    polar_up6,
    azimuth_up6,
    polar_first,
    polar_weights,
    azimuth_first,
    azimuth_weights,
    transfer5,
    sources5,
    offsets5,
    transfer4,
    sources4,
    offsets4,
):
    band_count = lax.axis_size("ang")
    block_count = lax.axis_size("clu")
    device_count = band_count * block_count
    device = lax.axis_index("clu") * band_count + lax.axis_index("ang")
    rows_six, cols_six = polar_up7.shape[0], azimuth_up7.shape[1]
    rows_five, cols_five = polar_up6.shape[0], azimuth_up6.shape[1]
    rows_four, cols_four = polar_first.shape[0], azimuth_first.shape[0]

    parents6 = patterns7.shape[0] // 8
    operator6 = polar_operator(polar_up7, (-1.0, 1.0), rows_six)[None]
    (level6,) = aggregate(
        patterns7.reshape((parents6, 2, 4) + patterns7.shape[1:]),
        operator6,
        azimuth_up7,
        transverse_factors(rows_six, cols_six),
        math.gcd(parents6, 8),
        True,
        None,
        "level6",
    )

    parents5 = parents6 // 8
    operator5 = polar_operator(polar_up6, (-1.0, 1.0), rows_five // 2)[None]
    level5, windows5 = aggregate(
        level6.reshape((parents5, 2, 4) + level6.shape[1:]),
        operator5,
        azimuth_up6,
        transverse_factors(rows_five, cols_five),
        1,
        True,
        (block_count, band_count),
        "level5",
    )
    windows5 = windows5.reshape((device_count,) + windows5.shape[2:])
    arrived5 = lax.all_to_all(windows5, ("clu", "ang"), 0, 0, tiled=True)
    arrived5 = arrived5.reshape((device_count * parents5,) + arrived5.shape[2:])

    four_taps = jnp.arange(4, dtype=jnp.int32)[None, :]
    polar_matrix = stencil_matrix(polar_first[:, None] + four_taps, polar_weights, rows_five)
    azimuth_matrix = stencil_matrix(
        (azimuth_first[:, None] + four_taps) % cols_five, azimuth_weights, cols_five
    ).T.astype(jnp.bfloat16)
    parts = parents5 // 4
    operators4 = []
    for part in range(parts):
        sign = (2 * ((device * parts + part) % 2) - 1).astype(jnp.float32)
        operators4.append(polar_operator(polar_matrix, (sign,), rows_four // 4))
    (windows4,) = aggregate(
        level5.reshape((parts, 1, 4) + level5.shape[1:]),
        jnp.stack(operators4),
        azimuth_matrix,
        transverse_factors(rows_four, cols_four),
        1,
        False,
        (block_count, band_count),
        "level4",
    )
    windows4 = windows4.reshape((device_count,) + windows4.shape[2:])
    arrived4 = lax.all_to_all(windows4, ("clu", "ang"), 0, 0, tiled=True)
    arrived4 = arrived4.reshape((device_count * parts,) + arrived4.shape[2:])

    translated5 = translate(
        arrived5, transfer5, sources5, offsets5, transfer5.shape[2], 1, "translate5"
    )
    translated4 = translate(arrived4, transfer4, sources4, offsets4, 16, 2, "translate4")
    return translated5, translated4


def solution(mesh):
    in_specs = (
        P(("clu", "ang"), None, None, None),
        P(),
        P(),
        P(),
        P(),
        P(),
        P(),
        P(),
        P(),
        P(None, None, "ang", "clu"),
        P(),
        P(),
        P(None, None, "ang", "clu"),
        P(),
        P(),
    )
    out_specs = (P(None, None, "ang", "clu"), P(None, None, "ang", "clu"))
    return jax.shard_map(shards, mesh=mesh, in_specs=in_specs, out_specs=out_specs, check_vma=False)
```

```python
import math

import jax
import jax.numpy as jnp
import numpy as np
from jax import lax
from jax.experimental import pallas as pl
from jax.experimental.pallas import tpu as pltpu
from jax.sharding import PartitionSpec as P

VMEM_LIMIT = 58 * 1024 * 1024
REGROUPS = 2


def sample_angles(rows, cols):
    polar = (np.arange(rows) + 0.5) * (np.pi / rows)
    azimuth = np.arange(cols) * (2.0 * np.pi / cols)
    return polar, azimuth


def transverse_factors(rows, cols):
    polar, azimuth = sample_angles(rows, cols)
    first = rows / 8.0 * np.sin(polar)[:, None] * np.cos(azimuth)[None, :]
    second = rows / 8.0 * np.sin(polar)[:, None] * np.sin(azimuth)[None, :]
    return np.stack(
        [
            np.cos(first) * np.cos(second),
            np.sin(first) * np.cos(second),
            np.cos(first) * np.sin(second),
            np.sin(first) * np.sin(second),
        ]
    ).astype(np.float32)


def polar_operator(matrix, signs, chunk):
    rows, taps = matrix.shape
    polar, _ = sample_angles(rows, 1)
    axial = rows / 8.0 * np.cos(polar)
    in_phase = matrix.astype(jnp.float32) * np.cos(axial).astype(np.float32)[:, None]
    quadrature = matrix.astype(jnp.float32) * np.sin(axial).astype(np.float32)[:, None]
    real_row = []
    imag_row = []
    for sign in signs:
        real_row += [in_phase, -sign * quadrature]
        imag_row += [sign * quadrature, in_phase]
    whole = jnp.stack([jnp.concatenate(real_row, axis=1), jnp.concatenate(imag_row, axis=1)])
    whole = whole.reshape(2, rows // chunk, chunk, 2 * len(signs) * taps)
    whole = whole.transpose(1, 0, 2, 3)
    return whole.reshape(rows // chunk, 2 * chunk, -1).astype(jnp.bfloat16)


def sign_sums(h, cols):
    h0, h1, h2, h3 = [h[:, k * cols : (k + 1) * cols] for k in range(4)]
    low_sum, low_diff = h0 + h1, h1 - h0
    high_sum, high_diff = h2 + h3, h3 - h2
    return jnp.concatenate(
        [
            (low_sum + high_sum).astype(jnp.bfloat16),
            (low_diff + high_diff).astype(jnp.bfloat16),
            (high_sum - low_sum).astype(jnp.bfloat16),
            (high_diff - low_diff).astype(jnp.bfloat16),
        ],
        axis=0,
    )


def apply_factors(y, chunk, factors):
    part = [y[k * chunk : (k + 1) * chunk] for k in range(8)]
    f0, f1, f2, f3 = factors
    real = f0 * part[0] - f1 * part[3] - f2 * part[5] - f3 * part[6]
    imag = f0 * part[1] + f1 * part[2] + f2 * part[4] - f3 * part[7]
    return real.astype(jnp.bfloat16), imag.astype(jnp.bfloat16)


def aggregate_kernel(pairs, width, split, x_ref, m_ref, b_ref, t_ref, o_ref):
    parents = x_ref.shape[0]
    rows2, cols = x_ref.shape[3] * x_ref.shape[4], x_ref.shape[5]
    chunk = t_ref.shape[1]
    steps = b_ref.shape[1] // width

    def one_parent(p):
        halves = []
        for child in range(4):
            stacked = [x_ref[p, s, child].reshape(rows2, cols) for s in range(pairs)]
            halves.append(jnp.concatenate(stacked, axis=0))
        joined = jnp.concatenate(halves, axis=1)
        h = jnp.dot(m_ref[0], joined, preferred_element_type=jnp.float32)
        sums = sign_sums(h, cols)

        def columns(j, start):
            cut = pl.ds(start, width)
            y = jnp.dot(sums, b_ref[:, cut], preferred_element_type=jnp.float32)
            both = apply_factors(y, chunk, [t_ref[k, :, cut] for k in range(4)])
            for c in range(2):
                if split:
                    band_rows, block_cols = o_ref.shape[4], o_ref.shape[5]
                    for q in range(width // block_cols):
                        for band in range(chunk // band_rows):
                            o_ref[j * (width // block_cols) + q, band, p, c] = both[c][
                                band * band_rows : (band + 1) * band_rows,
                                q * block_cols : (q + 1) * block_cols,
                            ]
                else:
                    o_ref[p, c, :, cut] = both[c]

        if steps == 1:
            columns(0, 0)
        else:

            @pl.loop(0, steps)
            def _(j):
                columns(j, pl.multiple_of(j * width, width))

    if parents == 1:
        one_parent(0)
    else:

        @pl.loop(0, parents, unroll=2)
        def _(p):
            one_parent(p)


def aggregate(children, operator, azimuth, factors, first, parents, group, split, name):
    _, pairs, _, _, taps, cols = children.shape
    chunks, chunk2, depth = operator.shape
    chunk = chunk2 // 2
    rows, out_cols = factors.shape[1], factors.shape[2]
    width = min(256, out_cols)
    if split is None:
        out_shape = jax.ShapeDtypeStruct((parents, 2, rows, out_cols), jnp.bfloat16)
        out_spec = pl.BlockSpec((group, 2, chunk, out_cols), lambda p, u: (p, 0, u, 0))
    else:
        blocks, bands = split
        band_rows, block_cols = rows // bands, out_cols // blocks
        width = max(width, block_cols)
        out_shape = jax.ShapeDtypeStruct(
            (blocks, bands, parents, 2, band_rows, block_cols), jnp.bfloat16
        )
        out_spec = pl.BlockSpec(
            (blocks, chunk // band_rows, group, 2, band_rows, block_cols),
            lambda p, u: (0, u, p, 0, 0, 0),
        )

    def body(*refs):
        aggregate_kernel(pairs, width, split is not None, *refs)

    skip = first // group
    flops = 2 * parents * chunks * 4 * (chunk2 * depth * cols + chunk2 * cols * out_cols)
    moved = 2 * parents * (16 * taps * cols + 2 * rows * out_cols) + 4 * factors.size
    return pl.pallas_call(
        body,
        grid=(parents // group, chunks),
        in_specs=[
            pl.BlockSpec((group, pairs, 4, 2, taps, cols), lambda p, u: (p + skip, 0, 0, 0, 0, 0)),
            pl.BlockSpec((1, chunk2, depth), lambda p, u: (u, 0, 0)),
            pl.BlockSpec(azimuth.shape, lambda p, u: (0, 0)),
            pl.BlockSpec((4, chunk, out_cols), lambda p, u: (0, u, 0)),
        ],
        out_specs=out_spec,
        out_shape=out_shape,
        compiler_params=pltpu.CompilerParams(vmem_limit_bytes=VMEM_LIMIT),
        cost_estimate=pl.CostEstimate(flops=flops, bytes_accessed=moved, transcendentals=0),
        name=name,
    )(children, operator, azimuth, factors)


def halfway_kernel(m_ref, e_ref, *refs):
    *inputs, h_ref, g_ref = refs
    count = len(inputs) // 2
    parents, _, held, _, rows, cols = inputs[0].shape
    edge_rows = inputs[count].shape[4]

    @pl.loop(0, parents, unroll=2)
    def _(p):
        siblings = []
        for c in range(count):
            for i in range(held):
                pieces = [inputs[c][p, s, i].reshape(2 * rows, cols) for s in range(2)]
                pieces += [
                    inputs[count + c][p, s, i].reshape(2 * edge_rows, cols) for s in range(2)
                ]
                siblings.append(jnp.concatenate(pieces, axis=0))
        joined = jnp.concatenate(siblings, axis=1)
        h = jnp.dot(m_ref[...], joined, preferred_element_type=jnp.float32)
        sums = sign_sums(h, cols)
        h_ref[p] = sums
        edges = lax.dot_general(
            e_ref[...], sums, (((1,), (1,)), ((), ())), preferred_element_type=jnp.float32
        )
        g_ref[p] = edges.astype(jnp.bfloat16)


def halfway(mains, edges, operator, picker):
    count = len(mains)
    parents, _, held, _, rows, cols = mains[0].shape
    edge_rows = edges[0].shape[4]
    group = math.gcd(parents, 4)
    out_rows = 4 * operator.shape[0]
    return pl.pallas_call(
        halfway_kernel,
        grid=(parents // group,),
        in_specs=[
            pl.BlockSpec(operator.shape, lambda p: (0, 0)),
            pl.BlockSpec(picker.shape, lambda p: (0, 0)),
        ]
        + [pl.BlockSpec((group, 2, held, 2, rows, cols), lambda p: (p, 0, 0, 0, 0, 0))] * count
        + [pl.BlockSpec((group, 2, held, 2, edge_rows, cols), lambda p: (p, 0, 0, 0, 0, 0))]
        * count,
        out_specs=[
            pl.BlockSpec((group, out_rows, cols), lambda p: (p, 0, 0)),
            pl.BlockSpec((group, picker.shape[0], out_rows), lambda p: (p, 0, 0)),
        ],
        out_shape=[
            jax.ShapeDtypeStruct((parents, out_rows, cols), jnp.bfloat16),
            jax.ShapeDtypeStruct((parents, picker.shape[0], out_rows), jnp.bfloat16),
        ],
        compiler_params=pltpu.CompilerParams(vmem_limit_bytes=VMEM_LIMIT),
        cost_estimate=pl.CostEstimate(
            flops=2 * parents * operator.size * 4 * cols,
            bytes_accessed=4 * parents * out_rows * cols,
            transcendentals=0,
        ),
        name="halfway4",
    )(operator, picker, *mains, *edges)


def phi_kernel(h_ref, low_ref, high_ref, b_ref, e_ref, t_ref, o_ref):
    parents = h_ref.shape[0]
    chunk = t_ref.shape[1]

    @pl.loop(0, parents, unroll=2)
    def _(p):
        outside = jnp.concatenate([low_ref[p], high_ref[p]], axis=0)
        y = jnp.dot(h_ref[p], b_ref[...], preferred_element_type=jnp.float32)
        y = y + lax.dot_general(
            outside, e_ref[...], (((0,), (0,)), ((), ())), preferred_element_type=jnp.float32
        )
        both = apply_factors(y, chunk, [t_ref[k] for k in range(4)])
        for c in range(2):
            o_ref[p, c] = both[c]


def interpolate_phi(h, low, high, azimuth, azimuth_edge, factors):
    parents, rows8, cols = h.shape
    _, rows, out_cols = factors.shape
    group = math.gcd(parents, 4)
    edge_spec = pl.BlockSpec((group,) + low.shape[1:], lambda p: (p, 0, 0))
    return pl.pallas_call(
        phi_kernel,
        grid=(parents // group,),
        in_specs=[
            pl.BlockSpec((group, rows8, cols), lambda p: (p, 0, 0)),
            edge_spec,
            edge_spec,
            pl.BlockSpec(azimuth.shape, lambda p: (0, 0)),
            pl.BlockSpec(azimuth_edge.shape, lambda p: (0, 0)),
            pl.BlockSpec(factors.shape, lambda p: (0, 0, 0)),
        ],
        out_specs=pl.BlockSpec((group, 2, rows, out_cols), lambda p: (p, 0, 0, 0)),
        out_shape=jax.ShapeDtypeStruct((parents, 2, rows, out_cols), jnp.bfloat16),
        compiler_params=pltpu.CompilerParams(vmem_limit_bytes=VMEM_LIMIT),
        cost_estimate=pl.CostEstimate(
            flops=2 * parents * rows8 * (cols + 16) * out_cols,
            bytes_accessed=4 * parents * rows8 * cols,
            transcendentals=0,
        ),
        name="level4",
    )(h, low, high, azimuth, azimuth_edge, factors)


def translate_kernel(slots, src, off, cnt, t_ref, *refs):
    *inputs, o_ref, held = refs
    targets = o_ref.shape[0]
    sources = held.shape[0] - 1
    senders, part = inputs[0].shape[:2]
    held[sources] = jnp.zeros(held.shape[1:], held.dtype)

    @pl.loop(0, senders)
    def _(s):
        for c, x_ref in enumerate(inputs):
            for i in range(part):
                held[(s * len(inputs) + c) * part + i] = x_ref[s, i]

    def gather(t, live):
        real = imag = None
        for first in range(0, live, 4):
            group_real = group_imag = None
            for j in range(first, min(first + 4, live)):
                picked = src[t * slots + j]
                chosen = off[t * slots + j]
                pr, pi = held[picked, 0], held[picked, 1]
                fr, fi = t_ref[chosen, 0], t_ref[chosen, 1]
                term_real = fr * pr - fi * pi
                term_imag = fr * pi + fi * pr
                group_real = term_real if group_real is None else group_real + term_real
                group_imag = term_imag if group_imag is None else group_imag + term_imag
            group_real = group_real.astype(jnp.float32)
            group_imag = group_imag.astype(jnp.float32)
            real = group_real if real is None else real + group_real
            imag = group_imag if imag is None else imag + group_imag
        o_ref[t, 0] = real.astype(o_ref.dtype)
        o_ref[t, 1] = imag.astype(o_ref.dtype)

    ends = sorted({min(slots, -(-slots * k // 16) * 4) for k in (2, 3)} | {slots})

    @pl.loop(0, targets)
    def _(t):
        live = cnt[t]
        lower = -1
        for end in ends:

            @pl.when(jnp.logical_and(live > lower, live <= end))
            def _(end=end):
                gather(t, end)

            lower = end


def translate(patterns, table, sources, displacements, row_chunk, name):
    targets, slots = sources.shape
    displacement_count, _, rows, cols = table.shape
    senders, part = patterns[0].shape[:2]
    held_count = senders * part * len(patterns)
    live = sources >= 0
    src = jnp.where(live, sources, held_count).reshape(-1)
    off = jnp.maximum(displacements, 0).reshape(-1)
    cnt = jnp.sum(live.astype(jnp.int32), axis=1)

    def body(*refs):
        translate_kernel(slots, *refs)

    return pl.pallas_call(
        body,
        grid_spec=pltpu.PrefetchScalarGridSpec(
            num_scalar_prefetch=3,
            grid=(rows // row_chunk,),
            in_specs=[
                pl.BlockSpec((displacement_count, 2, row_chunk, cols), lambda r, *_: (0, 0, r, 0)),
            ]
            + [pl.BlockSpec((senders, part, 2, row_chunk, cols), lambda r, *_: (0, 0, 0, r, 0))]
            * len(patterns),
            out_specs=pl.BlockSpec((targets, 2, row_chunk, cols), lambda r, *_: (0, 0, r, 0)),
            scratch_shapes=[pltpu.VMEM((held_count + 1, 2, row_chunk, cols), jnp.bfloat16)],
        ),
        out_shape=jax.ShapeDtypeStruct((targets, 2, rows, cols), jnp.bfloat16),
        compiler_params=pltpu.CompilerParams(vmem_limit_bytes=VMEM_LIMIT),
        cost_estimate=pl.CostEstimate(
            flops=8 * targets * slots * rows * cols,
            bytes_accessed=2 * (2 * targets * 2 * rows * cols + table.size),
            transcendentals=0,
        ),
        name=name,
    )(src, off, cnt, table, *patterns)


def stencil_matrix(tap_index, weights, column_count):
    matches = (
        tap_index[:, :, None] == jnp.arange(column_count, dtype=jnp.int32)[None, None, :]
    ).astype(jnp.float32)
    return jnp.sum(weights.astype(jnp.float32)[:, :, None] * matches, axis=1)


def shards(
    patterns7,
    polar_up7,
    azimuth_up7,
    polar_up6,
    azimuth_up6,
    polar_first,
    polar_weights,
    azimuth_first,
    azimuth_weights,
    transfer5,
    sources5,
    offsets5,
    transfer4,
    sources4,
    offsets4,
):
    band_count = lax.axis_size("ang")
    block_count = lax.axis_size("clu")
    device_count = band_count * block_count
    band = lax.axis_index("ang")
    block = lax.axis_index("clu")
    rows_six, cols_six = polar_up7.shape[0], azimuth_up7.shape[1]
    rows_five, cols_five = polar_up6.shape[0], azimuth_up6.shape[1]
    rows_four, cols_four = polar_first.shape[0], azimuth_first.shape[0]
    source_rows, source_cols = rows_five // band_count, cols_five // block_count
    band_rows, block_cols = rows_four // band_count, cols_four // block_count

    parents6 = patterns7.shape[0] // 8
    parents5 = parents6 // 8
    assert parents5 == 4
    part = parents5 // REGROUPS
    operator6 = polar_operator(polar_up7, (-1.0, 1.0), rows_six)
    operator5 = polar_operator(polar_up6, (-1.0, 1.0), rows_five // 2)
    children7 = patterns7.reshape((parents6, 2, 4) + patterns7.shape[1:])
    arrived5 = []
    for step in range(REGROUPS):
        level6 = aggregate(
            children7,
            operator6,
            azimuth_up7,
            transverse_factors(rows_six, cols_six),
            step * part * 8,
            part * 8,
            8,
            None,
            "level6",
        )
        windows5 = aggregate(
            level6.reshape((part, 2, 4) + level6.shape[1:]),
            operator5,
            azimuth_up6,
            transverse_factors(rows_five, cols_five),
            0,
            part,
            1,
            (block_count, band_count),
            "level5",
        )
        windows5 = windows5.reshape((device_count,) + windows5.shape[2:])
        arrived5.append(lax.all_to_all(windows5, ("clu", "ang"), 0, 0, tiled=True))

    upward = [(i, i + 1) for i in range(band_count - 1)]
    downward = [(i + 1, i) for i in range(band_count - 1)]
    edges5 = []
    for arrived in arrived5:
        low = lax.ppermute(arrived[:, :, :, source_rows - 3 :], "ang", upward)
        high = lax.ppermute(arrived[:, :, :, :3], "ang", downward)
        fill = jnp.zeros(arrived.shape[:3] + (10, source_cols), jnp.bfloat16)
        edges5.append(jnp.concatenate([low, high, fill], axis=3))

    four_taps = jnp.arange(4, dtype=jnp.int32)[None, :]
    polar_local = (
        lax.dynamic_slice_in_dim(polar_first, band * band_rows, band_rows, 0)
        - band * source_rows
        + 3
    )
    polar_matrix = stencil_matrix(
        polar_local[:, None] + four_taps,
        lax.dynamic_slice_in_dim(polar_weights, band * band_rows, band_rows, 0),
        source_rows + 6,
    )
    azimuth_local = (
        lax.dynamic_slice_in_dim(azimuth_first, block * block_cols, block_cols, 0)
        - block * source_cols
        + 3
    ) % cols_five
    azimuth_matrix = stencil_matrix(
        azimuth_local[:, None] + four_taps,
        lax.dynamic_slice_in_dim(azimuth_weights, block * block_cols, block_cols, 0),
        source_cols + 6,
    ).T.astype(jnp.bfloat16)

    axial = rows_four / 8.0 * np.cos(sample_angles(rows_four, 1)[0])
    cosine = lax.dynamic_slice_in_dim(
        jnp.asarray(np.cos(axial).astype(np.float32)), band * band_rows, band_rows, 0
    )
    sine = lax.dynamic_slice_in_dim(
        jnp.asarray(np.sin(axial).astype(np.float32)), band * band_rows, band_rows, 0
    )
    whole = polar_matrix[:, 3 : 3 + source_rows]
    edge = jnp.concatenate(
        [
            polar_matrix[:, :3],
            polar_matrix[:, 3 + source_rows :],
            jnp.zeros((band_rows, 10), jnp.float32),
        ],
        axis=1,
    )
    real_row = []
    imag_row = []
    for matrix in (whole, edge):
        in_phase, quadrature = matrix * cosine[:, None], matrix * sine[:, None]
        for sign in (-1.0, 1.0):
            real_row += [in_phase, -sign * quadrature]
            imag_row += [sign * quadrature, in_phase]
    operator4 = jnp.concatenate(
        [jnp.concatenate(real_row, axis=1), jnp.concatenate(imag_row, axis=1)], axis=0
    ).astype(jnp.bfloat16)
    picker = np.zeros((8, source_cols), np.float32)
    for k in range(3):
        picker[k, k] = 1.0
        picker[3 + k, source_cols - 3 + k] = 1.0
    shape4 = (device_count // 2, 2, part, 2)
    halfway4, edges4 = halfway(
        [arrived.reshape(shape4 + arrived.shape[3:]) for arrived in arrived5],
        [edges.reshape(shape4 + edges.shape[3:]) for edges in edges5],
        operator4,
        jnp.asarray(picker, jnp.bfloat16),
    )
    around = [(i, (i + 1) % block_count) for i in range(block_count)]
    from_low = lax.ppermute(edges4, "clu", around)
    from_high = lax.ppermute(edges4, "clu", [(b, a) for a, b in around])
    azimuth_edge = jnp.concatenate(
        [
            jnp.zeros((3, block_cols), jnp.bfloat16),
            azimuth_matrix[:3],
            jnp.zeros((2, block_cols), jnp.bfloat16),
            azimuth_matrix[3 + source_cols :],
            jnp.zeros((5, block_cols), jnp.bfloat16),
        ],
        axis=0,
    )
    factors4 = lax.dynamic_slice(
        jnp.asarray(transverse_factors(rows_four, cols_four)),
        (0, band * band_rows, block * block_cols),
        (4, band_rows, block_cols),
    )
    translated5 = translate(
        arrived5, transfer5, sources5, offsets5, transfer5.shape[2], "translate5"
    )
    level4 = interpolate_phi(
        halfway4,
        from_low,
        from_high,
        azimuth_matrix[3 : 3 + source_cols],
        azimuth_edge,
        factors4,
    )
    translated4 = translate([level4[:, None]], transfer4, sources4, offsets4, 16, "translate4")
    return translated5, translated4


def solution(mesh):
    in_specs = (
        P(("clu", "ang"), None, None, None),
        P(),
        P(),
        P(),
        P(),
        P(),
        P(),
        P(),
        P(),
        P(None, None, "ang", "clu"),
        P(),
        P(),
        P(None, None, "ang", "clu"),
        P(),
        P(),
    )
    out_specs = (P(None, None, "ang", "clu"), P(None, None, "ang", "clu"))
    return jax.shard_map(shards, mesh=mesh, in_specs=in_specs, out_specs=out_specs, check_vma=False)
```

```python
import math

import jax
import jax.numpy as jnp
import numpy as np
from jax import lax
from jax.experimental import pallas as pl
from jax.experimental.pallas import tpu as pltpu
from jax.sharding import PartitionSpec as P

VMEM_LIMIT = 58 * 1024 * 1024


def sample_angles(rows, cols):
    polar = (np.arange(rows) + 0.5) * (np.pi / rows)
    azimuth = np.arange(cols) * (2.0 * np.pi / cols)
    return polar, azimuth


def transverse_factors(rows, cols):
    polar, azimuth = sample_angles(rows, cols)
    first = rows / 8.0 * np.sin(polar)[:, None] * np.cos(azimuth)[None, :]
    second = rows / 8.0 * np.sin(polar)[:, None] * np.sin(azimuth)[None, :]
    return np.stack(
        [
            np.cos(first) * np.cos(second),
            np.sin(first) * np.cos(second),
            np.cos(first) * np.sin(second),
            np.sin(first) * np.sin(second),
        ]
    ).astype(np.float32)


def polar_operator(matrix, signs, chunk):
    rows, taps = matrix.shape
    polar, _ = sample_angles(rows, 1)
    axial = rows / 8.0 * np.cos(polar)
    in_phase = matrix.astype(jnp.float32) * np.cos(axial).astype(np.float32)[:, None]
    quadrature = matrix.astype(jnp.float32) * np.sin(axial).astype(np.float32)[:, None]
    real_row = []
    imag_row = []
    for sign in signs:
        real_row += [in_phase, -sign * quadrature]
        imag_row += [sign * quadrature, in_phase]
    whole = jnp.stack([jnp.concatenate(real_row, axis=1), jnp.concatenate(imag_row, axis=1)])
    whole = whole.reshape(2, rows // chunk, chunk, 2 * len(signs) * taps)
    whole = whole.transpose(1, 0, 2, 3)
    return whole.reshape(rows // chunk, 2 * chunk, -1).astype(jnp.bfloat16)


def sign_sums(h, cols):
    h0, h1, h2, h3 = [h[:, k * cols : (k + 1) * cols] for k in range(4)]
    low_sum, low_diff = h0 + h1, h1 - h0
    high_sum, high_diff = h2 + h3, h3 - h2
    return jnp.concatenate(
        [
            (low_sum + high_sum).astype(jnp.bfloat16),
            (low_diff + high_diff).astype(jnp.bfloat16),
            (high_sum - low_sum).astype(jnp.bfloat16),
            (high_diff - low_diff).astype(jnp.bfloat16),
        ],
        axis=0,
    )


def apply_factors(y, chunk, factors):
    part = [y[k * chunk : (k + 1) * chunk] for k in range(8)]
    f0, f1, f2, f3 = factors
    real = f0 * part[0] - f1 * part[3] - f2 * part[5] - f3 * part[6]
    imag = f0 * part[1] + f1 * part[2] + f2 * part[4] - f3 * part[7]
    return real.astype(jnp.bfloat16), imag.astype(jnp.bfloat16)


def siblings(block, child, pairs):
    rows2, cols = block.shape[-3] * block.shape[-2], block.shape[-1]
    stacked = [block[4 * s + child].reshape(rows2, cols) for s in range(pairs)]
    return jnp.concatenate(stacked, axis=0)


def produce_kernel(
    clu, ang, x_ref, m6, b6, t6, m5, b5, t5, arrived, level6, windows, send_sem, recv_sem, own_sem
):
    step = pl.program_id(0)
    steps = pl.num_programs(0)
    devices = clu * ang
    me = lax.axis_index("clu") * ang + lax.axis_index("ang")

    @pl.when(step == 0)
    def _():
        barrier = pltpu.get_barrier_semaphore()

        @pl.loop(1, devices)
        def _(k):
            other = lax.rem(me + k, devices)
            pl.semaphore_signal(
                barrier,
                inc=1,
                device_id=(other // ang, lax.rem(other, ang)),
                device_id_type=pl.DeviceIdType.MESH,
            )

        pl.semaphore_wait(barrier, devices - 1)

    @pl.loop(0, 8, unroll=2)
    def _(p):
        cols = x_ref.shape[4]
        joined = jnp.concatenate([siblings(x_ref.at[p], o, 2) for o in range(4)], axis=1)
        h = jnp.dot(m6[...], joined, preferred_element_type=jnp.float32)
        sums = sign_sums(h, cols)
        y = jnp.dot(sums, b6[...], preferred_element_type=jnp.float32)
        both = apply_factors(y, t6.shape[1], [t6[k] for k in range(4)])
        for c in range(2):
            level6[p, c] = both[c]

    cols = level6.shape[3]
    chunks, chunk2 = m5.shape[:2]
    chunk = chunk2 // 2
    band_rows, block_cols = windows.shape[2], windows.shape[3]
    bands = chunk // band_rows
    width = min(256, b5.shape[1])

    @pl.loop(0, chunks)
    def _(u):
        joined = jnp.concatenate([siblings(level6, o, 2) for o in range(4)], axis=1)
        h = jnp.dot(m5[u], joined, preferred_element_type=jnp.float32)
        sums = sign_sums(h, cols)
        for j in range(b5.shape[1] // width):
            cut = slice(j * width, (j + 1) * width)
            y = jnp.dot(sums, b5[:, cut], preferred_element_type=jnp.float32)
            rows = pl.ds(pl.multiple_of(u * chunk, chunk), chunk)
            both = apply_factors(y, chunk, [t5[k, rows, cut] for k in range(4)])
            for c in range(2):
                for q in range(width // block_cols):
                    for band in range(bands):
                        target = (j * (width // block_cols) + q) * ang + u * bands + band
                        windows[step * devices + target, c] = both[c][
                            band * band_rows : (band + 1) * band_rows,
                            q * block_cols : (q + 1) * block_cols,
                        ]

    @pl.loop(1, devices)
    def _(k):
        other = lax.rem(me + k, devices)
        pltpu.make_async_remote_copy(
            src_ref=windows.at[step * devices + other],
            dst_ref=arrived.at[step * devices + me],
            send_sem=send_sem,
            recv_sem=recv_sem,
            device_id=(other // ang, lax.rem(other, ang)),
            device_id_type=pl.DeviceIdType.MESH,
        ).start()

    pltpu.make_async_copy(
        windows.at[step * devices + me], arrived.at[step * devices + me], own_sem.at[step]
    ).start()

    @pl.when(step == steps - 1)
    def _():
        away = pl.ds(0, 4 * (devices - 1))
        everything = pltpu.make_async_remote_copy(
            src_ref=windows.at[away],
            dst_ref=arrived.at[away],
            send_sem=send_sem,
            recv_sem=recv_sem,
            device_id=(lax.axis_index("clu"), lax.rem(lax.axis_index("ang") + 1, ang)),
            device_id_type=pl.DeviceIdType.MESH,
        )
        everything.wait_send()
        everything.wait_recv()
        for k in range(4):
            pltpu.make_async_copy(
                windows.at[k * devices + me], arrived.at[k * devices + me], own_sem.at[k]
            ).wait()


def produce(children, operators, azimuths, factors, clu, ang):
    parents = children.shape[0] // 64
    rows, cols = factors[1].shape[1:]
    window = (2, rows // ang, cols // clu)
    devices = clu * ang

    def body(*refs):
        produce_kernel(clu, ang, *refs)

    def whole(array):
        zeros = (0,) * array.ndim
        return pl.BlockSpec(array.shape, lambda p: zeros)

    arguments = [operators[0][0], azimuths[0], factors[0], operators[1], azimuths[1], factors[1]]
    return pl.pallas_call(
        body,
        grid=(parents,),
        in_specs=[pl.BlockSpec((8, 8) + children.shape[1:], lambda p: (p, 0, 0, 0, 0))]
        + [whole(array) for array in arguments],
        out_specs=pl.BlockSpec(memory_space=pl.ANY),
        out_shape=jax.ShapeDtypeStruct((parents * devices,) + window, jnp.bfloat16),
        scratch_shapes=[
            pltpu.VMEM((8, 2) + factors[0].shape[1:], jnp.bfloat16),
            pltpu.VMEM((parents * devices,) + window, jnp.bfloat16),
            pltpu.SemaphoreType.DMA,
            pltpu.SemaphoreType.DMA,
            pltpu.SemaphoreType.DMA((4,)),
        ],
        compiler_params=pltpu.CompilerParams(
            vmem_limit_bytes=VMEM_LIMIT, collective_id=0, has_side_effects=True
        ),
        name="produce",
    )(children.reshape((-1, 8) + children.shape[1:]), *arguments)


def halfway_kernel(m_ref, e_ref, x_ref, edge_ref, h_ref, g_ref):
    _, parents, _, _, rows, cols = x_ref.shape
    edge_rows = edge_ref.shape[4]

    @pl.loop(0, parents, unroll=2)
    def _(p):
        family = []
        for o in range(4):
            pieces = [x_ref[o, p, s].reshape(2 * rows, cols) for s in range(2)]
            pieces += [edge_ref[o, p, s].reshape(2 * edge_rows, cols) for s in range(2)]
            family.append(jnp.concatenate(pieces, axis=0))
        joined = jnp.concatenate(family, axis=1)
        h = jnp.dot(m_ref[...], joined, preferred_element_type=jnp.float32)
        sums = sign_sums(h, cols)
        h_ref[p] = sums
        edges = lax.dot_general(
            e_ref[...], sums, (((1,), (1,)), ((), ())), preferred_element_type=jnp.float32
        )
        g_ref[p] = edges.astype(jnp.bfloat16)


def halfway(main, edges, operator, picker):
    _, parents, _, _, rows, cols = main.shape
    edge_rows = edges.shape[4]
    group = math.gcd(parents, 4)
    out_rows = 4 * operator.shape[0]
    return pl.pallas_call(
        halfway_kernel,
        grid=(parents // group,),
        in_specs=[
            pl.BlockSpec(operator.shape, lambda p: (0, 0)),
            pl.BlockSpec(picker.shape, lambda p: (0, 0)),
            pl.BlockSpec((4, group, 2, 2, rows, cols), lambda p: (0, p, 0, 0, 0, 0)),
            pl.BlockSpec((4, group, 2, 2, edge_rows, cols), lambda p: (0, p, 0, 0, 0, 0)),
        ],
        out_specs=[
            pl.BlockSpec((group, out_rows, cols), lambda p: (p, 0, 0)),
            pl.BlockSpec((group, picker.shape[0], out_rows), lambda p: (p, 0, 0)),
        ],
        out_shape=[
            jax.ShapeDtypeStruct((parents, out_rows, cols), jnp.bfloat16),
            jax.ShapeDtypeStruct((parents, picker.shape[0], out_rows), jnp.bfloat16),
        ],
        compiler_params=pltpu.CompilerParams(vmem_limit_bytes=VMEM_LIMIT),
        cost_estimate=pl.CostEstimate(
            flops=2 * parents * operator.size * 4 * cols,
            bytes_accessed=4 * parents * out_rows * cols,
            transcendentals=0,
        ),
        name="halfway4",
    )(operator, picker, main, edges)


def phi_kernel(h_ref, low_ref, high_ref, b_ref, e_ref, t_ref, o_ref):
    parents = h_ref.shape[0]
    chunk = t_ref.shape[1]

    @pl.loop(0, parents, unroll=2)
    def _(p):
        outside = jnp.concatenate([low_ref[p], high_ref[p]], axis=0)
        y = jnp.dot(h_ref[p], b_ref[...], preferred_element_type=jnp.float32)
        y = y + lax.dot_general(
            outside, e_ref[...], (((0,), (0,)), ((), ())), preferred_element_type=jnp.float32
        )
        both = apply_factors(y, chunk, [t_ref[k] for k in range(4)])
        for c in range(2):
            o_ref[p, c] = both[c]


def interpolate_phi(h, low, high, azimuth, azimuth_edge, factors):
    parents, rows8, cols = h.shape
    _, rows, out_cols = factors.shape
    group = math.gcd(parents, 4)
    edge_spec = pl.BlockSpec((group,) + low.shape[1:], lambda p: (p, 0, 0))
    return pl.pallas_call(
        phi_kernel,
        grid=(parents // group,),
        in_specs=[
            pl.BlockSpec((group, rows8, cols), lambda p: (p, 0, 0)),
            edge_spec,
            edge_spec,
            pl.BlockSpec(azimuth.shape, lambda p: (0, 0)),
            pl.BlockSpec(azimuth_edge.shape, lambda p: (0, 0)),
            pl.BlockSpec(factors.shape, lambda p: (0, 0, 0)),
        ],
        out_specs=pl.BlockSpec((group, 2, rows, out_cols), lambda p: (p, 0, 0, 0)),
        out_shape=jax.ShapeDtypeStruct((parents, 2, rows, out_cols), jnp.bfloat16),
        compiler_params=pltpu.CompilerParams(vmem_limit_bytes=VMEM_LIMIT),
        cost_estimate=pl.CostEstimate(
            flops=2 * parents * rows8 * (cols + 16) * out_cols,
            bytes_accessed=4 * parents * rows8 * cols,
            transcendentals=0,
        ),
        name="level4",
    )(h, low, high, azimuth, azimuth_edge, factors)


def translate_kernel(src, off, x_ref, t_ref, o_ref, held):
    targets = o_ref.shape[0]
    slots = src.shape[1]
    parts, senders = x_ref.shape[:2]
    sources = parts * senders
    held[sources] = jnp.zeros(held.shape[1:], held.dtype)

    @pl.loop(0, senders)
    def _(s):
        for c in range(parts):
            held[s * parts + c] = x_ref[c, s]

    def gather(t, lower, end):
        real = imag = None
        for first in range(0, end, 4):
            group_real = group_imag = None
            for j in range(first, min(first + 4, end)):
                picked = src[t, j]
                chosen = off[t, j]
                if j > lower:
                    picked = jnp.where(picked < 0, sources, picked)
                    chosen = jnp.maximum(chosen, 0)
                pr, pi = held[picked, 0], held[picked, 1]
                fr, fi = t_ref[chosen, 0], t_ref[chosen, 1]
                term_real = fr * pr - fi * pi
                term_imag = fr * pi + fi * pr
                group_real = term_real if group_real is None else group_real + term_real
                group_imag = term_imag if group_imag is None else group_imag + term_imag
            group_real = group_real.astype(jnp.float32)
            group_imag = group_imag.astype(jnp.float32)
            real = group_real if real is None else real + group_real
            imag = group_imag if imag is None else imag + group_imag
        o_ref[t, 0] = real.astype(o_ref.dtype)
        o_ref[t, 1] = imag.astype(o_ref.dtype)

    ends = [end for end in (8, 12) if end < slots] + [slots]

    @pl.loop(0, targets)
    def _(t):
        lower = 0
        for end in ends:
            wanted = src[t, lower] >= 0
            if end < slots:
                wanted = jnp.logical_and(wanted, src[t, end] < 0)

            @pl.when(wanted)
            def _(lower=lower, end=end):
                gather(t, lower, end)

            lower = end


def translate(patterns, table, sources, displacements, row_chunk, name):
    targets, slots = sources.shape
    displacement_count, _, rows, cols = table.shape
    parts, senders = patterns.shape[:2]
    return pl.pallas_call(
        translate_kernel,
        grid_spec=pltpu.PrefetchScalarGridSpec(
            num_scalar_prefetch=2,
            grid=(rows // row_chunk,),
            in_specs=[
                pl.BlockSpec((parts, senders, 2, row_chunk, cols), lambda r, *_: (0, 0, 0, r, 0)),
                pl.BlockSpec((displacement_count, 2, row_chunk, cols), lambda r, *_: (0, 0, r, 0)),
            ],
            out_specs=pl.BlockSpec((targets, 2, row_chunk, cols), lambda r, *_: (0, 0, r, 0)),
            scratch_shapes=[pltpu.VMEM((parts * senders + 1, 2, row_chunk, cols), jnp.bfloat16)],
        ),
        out_shape=jax.ShapeDtypeStruct((targets, 2, rows, cols), jnp.bfloat16),
        compiler_params=pltpu.CompilerParams(vmem_limit_bytes=VMEM_LIMIT),
        cost_estimate=pl.CostEstimate(
            flops=8 * targets * slots * rows * cols,
            bytes_accessed=2 * (2 * targets * 2 * rows * cols + table.size),
            transcendentals=0,
        ),
        name=name,
    )(sources, displacements, patterns, table)


def stencil_matrix(tap_index, weights, column_count):
    matches = (
        tap_index[:, :, None] == jnp.arange(column_count, dtype=jnp.int32)[None, None, :]
    ).astype(jnp.float32)
    return jnp.sum(weights.astype(jnp.float32)[:, :, None] * matches, axis=1)


def shards(
    patterns7,
    polar_up7,
    azimuth_up7,
    polar_up6,
    azimuth_up6,
    polar_first,
    polar_weights,
    azimuth_first,
    azimuth_weights,
    transfer5,
    sources5,
    offsets5,
    transfer4,
    sources4,
    offsets4,
):
    band_count = lax.axis_size("ang")
    block_count = lax.axis_size("clu")
    device_count = band_count * block_count
    band = lax.axis_index("ang")
    block = lax.axis_index("clu")
    rows_six, cols_six = polar_up7.shape[0], azimuth_up7.shape[1]
    rows_five, cols_five = polar_up6.shape[0], azimuth_up6.shape[1]
    rows_four, cols_four = polar_first.shape[0], azimuth_first.shape[0]
    source_rows, source_cols = rows_five // band_count, cols_five // block_count
    band_rows, block_cols = rows_four // band_count, cols_four // block_count

    parents6 = patterns7.shape[0] // 8
    parents5 = parents6 // 8
    assert parents5 == 4
    arrived5 = produce(
        patterns7,
        (
            polar_operator(polar_up7, (-1.0, 1.0), rows_six),
            polar_operator(polar_up6, (-1.0, 1.0), rows_five // 2),
        ),
        (azimuth_up7, azimuth_up6),
        (transverse_factors(rows_six, cols_six), transverse_factors(rows_five, cols_five)),
        block_count,
        band_count,
    )
    arrived5 = arrived5.reshape((parents5, device_count) + arrived5.shape[1:])

    upward = [(i, i + 1) for i in range(band_count - 1)]
    downward = [(i + 1, i) for i in range(band_count - 1)]
    low = lax.ppermute(arrived5[:, :, :, source_rows - 3 :], "ang", upward)
    high = lax.ppermute(arrived5[:, :, :, :3], "ang", downward)
    fill = jnp.zeros(arrived5.shape[:3] + (10, source_cols), jnp.bfloat16)
    edges5 = jnp.concatenate([low, high, fill], axis=3)

    four_taps = jnp.arange(4, dtype=jnp.int32)[None, :]
    polar_local = (
        lax.dynamic_slice_in_dim(polar_first, band * band_rows, band_rows, 0)
        - band * source_rows
        + 3
    )
    polar_matrix = stencil_matrix(
        polar_local[:, None] + four_taps,
        lax.dynamic_slice_in_dim(polar_weights, band * band_rows, band_rows, 0),
        source_rows + 6,
    )
    azimuth_local = (
        lax.dynamic_slice_in_dim(azimuth_first, block * block_cols, block_cols, 0)
        - block * source_cols
        + 3
    ) % cols_five
    azimuth_matrix = stencil_matrix(
        azimuth_local[:, None] + four_taps,
        lax.dynamic_slice_in_dim(azimuth_weights, block * block_cols, block_cols, 0),
        source_cols + 6,
    ).T.astype(jnp.bfloat16)

    axial = rows_four / 8.0 * np.cos(sample_angles(rows_four, 1)[0])
    cosine = lax.dynamic_slice_in_dim(
        jnp.asarray(np.cos(axial).astype(np.float32)), band * band_rows, band_rows, 0
    )
    sine = lax.dynamic_slice_in_dim(
        jnp.asarray(np.sin(axial).astype(np.float32)), band * band_rows, band_rows, 0
    )
    whole = polar_matrix[:, 3 : 3 + source_rows]
    edge = jnp.concatenate(
        [
            polar_matrix[:, :3],
            polar_matrix[:, 3 + source_rows :],
            jnp.zeros((band_rows, 10), jnp.float32),
        ],
        axis=1,
    )
    real_row = []
    imag_row = []
    for matrix in (whole, edge):
        in_phase, quadrature = matrix * cosine[:, None], matrix * sine[:, None]
        for sign in (-1.0, 1.0):
            real_row += [in_phase, -sign * quadrature]
            imag_row += [sign * quadrature, in_phase]
    operator4 = jnp.concatenate(
        [jnp.concatenate(real_row, axis=1), jnp.concatenate(imag_row, axis=1)], axis=0
    ).astype(jnp.bfloat16)
    picker = np.zeros((8, source_cols), np.float32)
    for k in range(3):
        picker[k, k] = 1.0
        picker[3 + k, source_cols - 3 + k] = 1.0
    shape4 = (parents5, device_count // 2, 2, 2)
    halfway4, edges4 = halfway(
        arrived5.reshape(shape4 + arrived5.shape[3:]),
        edges5.reshape(shape4 + edges5.shape[3:]),
        operator4,
        jnp.asarray(picker, jnp.bfloat16),
    )
    around = [(i, (i + 1) % block_count) for i in range(block_count)]
    from_low = lax.ppermute(edges4, "clu", around)
    from_high = lax.ppermute(edges4, "clu", [(b, a) for a, b in around])
    azimuth_edge = jnp.concatenate(
        [
            jnp.zeros((3, block_cols), jnp.bfloat16),
            azimuth_matrix[:3],
            jnp.zeros((2, block_cols), jnp.bfloat16),
            azimuth_matrix[3 + source_cols :],
            jnp.zeros((5, block_cols), jnp.bfloat16),
        ],
        axis=0,
    )
    factors4 = lax.dynamic_slice(
        jnp.asarray(transverse_factors(rows_four, cols_four)),
        (0, band * band_rows, block * block_cols),
        (4, band_rows, block_cols),
    )
    translated5 = translate(
        arrived5, transfer5, sources5, offsets5, transfer5.shape[2], "translate5"
    )
    level4 = interpolate_phi(
        halfway4,
        from_low,
        from_high,
        azimuth_matrix[3 : 3 + source_cols],
        azimuth_edge,
        factors4,
    )
    translated4 = translate(level4[None], transfer4, sources4, offsets4, 16, "translate4")
    return translated5, translated4


def solution(mesh):
    in_specs = (
        P(("clu", "ang"), None, None, None),
        P(),
        P(),
        P(),
        P(),
        P(),
        P(),
        P(),
        P(),
        P(None, None, "ang", "clu"),
        P(),
        P(),
        P(None, None, "ang", "clu"),
        P(),
        P(),
    )
    out_specs = (P(None, None, "ang", "clu"), P(None, None, "ang", "clu"))
    return jax.shard_map(shards, mesh=mesh, in_specs=in_specs, out_specs=out_specs, check_vma=False)
```

```python
import math

import jax
import jax.numpy as jnp
import numpy as np
from jax import lax
from jax.experimental import pallas as pl
from jax.experimental.pallas import tpu as pltpu
from jax.sharding import PartitionSpec as P

VMEM_LIMIT = 58 * 1024 * 1024


def sample_angles(rows, cols):
    polar = (np.arange(rows) + 0.5) * (np.pi / rows)
    azimuth = np.arange(cols) * (2.0 * np.pi / cols)
    return polar, azimuth


def transverse_factors(rows, cols):
    polar, azimuth = sample_angles(rows, cols)
    first = rows / 8.0 * np.sin(polar)[:, None] * np.cos(azimuth)[None, :]
    second = rows / 8.0 * np.sin(polar)[:, None] * np.sin(azimuth)[None, :]
    return np.stack(
        [
            np.cos(first) * np.cos(second),
            np.sin(first) * np.cos(second),
            np.cos(first) * np.sin(second),
            np.sin(first) * np.sin(second),
        ]
    ).astype(np.float32)


def polar_operator(matrix, signs, chunk):
    rows, taps = matrix.shape
    polar, _ = sample_angles(rows, 1)
    axial = rows / 8.0 * np.cos(polar)
    in_phase = matrix.astype(jnp.float32) * np.cos(axial).astype(np.float32)[:, None]
    quadrature = matrix.astype(jnp.float32) * np.sin(axial).astype(np.float32)[:, None]
    real_row = []
    imag_row = []
    for sign in signs:
        real_row += [in_phase, -sign * quadrature]
        imag_row += [sign * quadrature, in_phase]
    whole = jnp.stack([jnp.concatenate(real_row, axis=1), jnp.concatenate(imag_row, axis=1)])
    whole = whole.reshape(2, rows // chunk, chunk, 2 * len(signs) * taps)
    whole = whole.transpose(1, 0, 2, 3)
    return whole.reshape(rows // chunk, 2 * chunk, -1).astype(jnp.bfloat16)


def sign_sums(h, cols):
    h0, h1, h2, h3 = [h[:, k * cols : (k + 1) * cols] for k in range(4)]
    low_sum, low_diff = h0 + h1, h1 - h0
    high_sum, high_diff = h2 + h3, h3 - h2
    return jnp.concatenate(
        [
            (low_sum + high_sum).astype(jnp.bfloat16),
            (low_diff + high_diff).astype(jnp.bfloat16),
            (high_sum - low_sum).astype(jnp.bfloat16),
            (high_diff - low_diff).astype(jnp.bfloat16),
        ],
        axis=0,
    )


def apply_factors(y, chunk, factors):
    part = [y[k * chunk : (k + 1) * chunk] for k in range(8)]
    f0, f1, f2, f3 = factors
    real = f0 * part[0] - f1 * part[3] - f2 * part[5] - f3 * part[6]
    imag = f0 * part[1] + f1 * part[2] + f2 * part[4] - f3 * part[7]
    return real.astype(jnp.bfloat16), imag.astype(jnp.bfloat16)


def siblings(block, child, pairs):
    rows2, cols = block.shape[-3] * block.shape[-2], block.shape[-1]
    stacked = [block[4 * s + child].reshape(rows2, cols) for s in range(pairs)]
    return jnp.concatenate(stacked, axis=0)


def produce_kernel(
    clu, ang, x_ref, m6, b6, t6, m5, b5, t5, arrived, level6, windows, send_sem, recv_sem, own_sem
):
    step = pl.program_id(0)
    steps = pl.num_programs(0)
    devices = clu * ang
    me = lax.axis_index("clu") * ang + lax.axis_index("ang")

    @pl.when(step == 0)
    def _():
        barrier = pltpu.get_barrier_semaphore()

        @pl.loop(1, devices)
        def _(k):
            other = lax.rem(me + k, devices)
            pl.semaphore_signal(
                barrier,
                inc=1,
                device_id=(other // ang, lax.rem(other, ang)),
                device_id_type=pl.DeviceIdType.MESH,
            )

        pl.semaphore_wait(barrier, devices - 1)

    @pl.loop(0, 8, unroll=2)
    def _(p):
        cols = x_ref.shape[4]
        joined = jnp.concatenate([siblings(x_ref.at[p], o, 2) for o in range(4)], axis=1)
        h = jnp.dot(m6[...], joined, preferred_element_type=jnp.float32)
        sums = sign_sums(h, cols)
        y = jnp.dot(sums, b6[...], preferred_element_type=jnp.float32)
        both = apply_factors(y, t6.shape[1], [t6[k] for k in range(4)])
        for c in range(2):
            level6[p, c] = both[c]

    cols = level6.shape[3]
    chunks, chunk2 = m5.shape[:2]
    chunk = chunk2 // 2
    band_rows, block_cols = windows.shape[2], windows.shape[3]
    bands = chunk // band_rows
    width = min(256, b5.shape[1])

    @pl.loop(0, chunks)
    def _(u):
        joined = jnp.concatenate([siblings(level6, o, 2) for o in range(4)], axis=1)
        h = jnp.dot(m5[u], joined, preferred_element_type=jnp.float32)
        sums = sign_sums(h, cols)
        for j in range(b5.shape[1] // width):
            cut = slice(j * width, (j + 1) * width)
            y = jnp.dot(sums, b5[:, cut], preferred_element_type=jnp.float32)
            rows = pl.ds(pl.multiple_of(u * chunk, chunk), chunk)
            both = apply_factors(y, chunk, [t5[k, rows, cut] for k in range(4)])
            for c in range(2):
                for q in range(width // block_cols):
                    for band in range(bands):
                        target = (j * (width // block_cols) + q) * ang + u * bands + band
                        windows[step * devices + target, c] = both[c][
                            band * band_rows : (band + 1) * band_rows,
                            q * block_cols : (q + 1) * block_cols,
                        ]

    @pl.loop(1, devices)
    def _(k):
        other = lax.rem(me + k, devices)
        pltpu.make_async_remote_copy(
            src_ref=windows.at[step * devices + other],
            dst_ref=arrived.at[step * devices + me],
            send_sem=send_sem,
            recv_sem=recv_sem,
            device_id=(other // ang, lax.rem(other, ang)),
            device_id_type=pl.DeviceIdType.MESH,
        ).start()

    pltpu.make_async_copy(
        windows.at[step * devices + me], arrived.at[step * devices + me], own_sem.at[step]
    ).start()

    @pl.when(step == steps - 1)
    def _():
        away = pl.ds(0, 4 * (devices - 1))
        everything = pltpu.make_async_remote_copy(
            src_ref=windows.at[away],
            dst_ref=arrived.at[away],
            send_sem=send_sem,
            recv_sem=recv_sem,
            device_id=(lax.axis_index("clu"), lax.rem(lax.axis_index("ang") + 1, ang)),
            device_id_type=pl.DeviceIdType.MESH,
        )
        everything.wait_send()
        everything.wait_recv()
        for k in range(4):
            pltpu.make_async_copy(
                windows.at[k * devices + me], arrived.at[k * devices + me], own_sem.at[k]
            ).wait()


def produce(children, operators, azimuths, factors, clu, ang):
    parents = children.shape[0] // 64
    rows, cols = factors[1].shape[1:]
    window = (2, rows // ang, cols // clu)
    devices = clu * ang

    def body(*refs):
        produce_kernel(clu, ang, *refs)

    def whole(array):
        zeros = (0,) * array.ndim
        return pl.BlockSpec(array.shape, lambda p: zeros)

    arguments = [operators[0][0], azimuths[0], factors[0], operators[1], azimuths[1], factors[1]]
    return pl.pallas_call(
        body,
        grid=(parents,),
        in_specs=[pl.BlockSpec((8, 8) + children.shape[1:], lambda p: (p, 0, 0, 0, 0))]
        + [whole(array) for array in arguments],
        out_specs=pl.BlockSpec(memory_space=pl.ANY),
        out_shape=jax.ShapeDtypeStruct((parents * devices,) + window, jnp.bfloat16),
        scratch_shapes=[
            pltpu.VMEM((8, 2) + factors[0].shape[1:], jnp.bfloat16),
            pltpu.VMEM((parents * devices,) + window, jnp.bfloat16),
            pltpu.SemaphoreType.DMA,
            pltpu.SemaphoreType.DMA,
            pltpu.SemaphoreType.DMA((4,)),
        ],
        compiler_params=pltpu.CompilerParams(
            vmem_limit_bytes=VMEM_LIMIT, collective_id=0, has_side_effects=True
        ),
        name="produce",
    )(children.reshape((-1, 8) + children.shape[1:]), *arguments)


def halfway_kernel(place, s_ref, e_ref, x_ref, edge_ref, h_ref, g_ref, m_ref):
    _, parents, _, _, rows, cols = x_ref.shape
    edge_rows = edge_ref.shape[4]
    band_rows = s_ref.shape[0]

    @pl.when(pl.program_id(0) == 0)
    def _():
        stencil = s_ref[...]
        first = stencil[:, 0:1].astype(jnp.int32) - place[0] * rows

        def matrix(position):
            total = jnp.zeros(position.shape, jnp.float32)
            for k in range(4):
                total = total + jnp.where(position == first + k, stencil[:, 1 + k : 2 + k], 0.0)
            return total

        inner = lax.broadcasted_iota(jnp.int32, (band_rows, rows), 1)
        outer = lax.broadcasted_iota(jnp.int32, (band_rows, edge_rows), 1)
        outer = jnp.where(outer < 3, outer - 3, jnp.where(outer < 6, outer + rows - 3, -100))
        start = 0
        for whole in (matrix(inner), matrix(outer)):
            in_phase = (whole * stencil[:, 5:6]).astype(jnp.bfloat16)
            quadrature = (whole * stencil[:, 6:7]).astype(jnp.bfloat16)
            width = whole.shape[1]
            for left, right in ((in_phase, quadrature), (in_phase, -quadrature)):
                m_ref[:band_rows, start : start + width] = left
                m_ref[band_rows:, start : start + width] = -right
                m_ref[:band_rows, start + width : start + 2 * width] = right
                m_ref[band_rows:, start + width : start + 2 * width] = left
                start += 2 * width

    @pl.loop(0, parents, unroll=2)
    def _(p):
        family = []
        for o in range(4):
            pieces = [x_ref[o, p, s].reshape(2 * rows, cols) for s in range(2)]
            pieces += [edge_ref[o, p, s].reshape(2 * edge_rows, cols) for s in range(2)]
            family.append(jnp.concatenate(pieces, axis=0))
        joined = jnp.concatenate(family, axis=1)
        h = jnp.dot(m_ref[...], joined, preferred_element_type=jnp.float32)
        sums = sign_sums(h, cols)
        h_ref[p] = sums
        edges = lax.dot_general(
            e_ref[...], sums, (((1,), (1,)), ((), ())), preferred_element_type=jnp.float32
        )
        g_ref[p] = edges.astype(jnp.bfloat16)


def halfway(main, edges, stencil, picker, place, band_rows):
    _, parents, _, _, rows, cols = main.shape
    edge_rows = edges.shape[4]
    group = math.gcd(parents, 4)
    out_rows = 8 * band_rows
    depth = 4 * (rows + edge_rows)
    return pl.pallas_call(
        halfway_kernel,
        grid_spec=pltpu.PrefetchScalarGridSpec(
            num_scalar_prefetch=1,
            grid=(parents // group,),
            in_specs=[
                pl.BlockSpec((band_rows, stencil.shape[1]), lambda p, at: (at[0], 0)),
                pl.BlockSpec(picker.shape, lambda p, at: (0, 0)),
                pl.BlockSpec((4, group, 2, 2, rows, cols), lambda p, at: (0, p, 0, 0, 0, 0)),
                pl.BlockSpec((4, group, 2, 2, edge_rows, cols), lambda p, at: (0, p, 0, 0, 0, 0)),
            ],
            out_specs=[
                pl.BlockSpec((group, out_rows, cols), lambda p, at: (p, 0, 0)),
                pl.BlockSpec((group, picker.shape[0], out_rows), lambda p, at: (p, 0, 0)),
            ],
            scratch_shapes=[pltpu.VMEM((2 * band_rows, depth), jnp.bfloat16)],
        ),
        out_shape=[
            jax.ShapeDtypeStruct((parents, out_rows, cols), jnp.bfloat16),
            jax.ShapeDtypeStruct((parents, picker.shape[0], out_rows), jnp.bfloat16),
        ],
        compiler_params=pltpu.CompilerParams(vmem_limit_bytes=VMEM_LIMIT),
        cost_estimate=pl.CostEstimate(
            flops=2 * parents * out_rows * depth * cols,
            bytes_accessed=4 * parents * out_rows * cols,
            transcendentals=0,
        ),
        name="halfway4",
    )(place, stencil, picker, main, edges)


def phi_kernel(circle, place, h_ref, low_ref, high_ref, f_ref, w_ref, t_ref, o_ref, b_ref, e_ref):
    parents = h_ref.shape[0]
    chunk = t_ref.shape[1]
    cols, out_cols = b_ref.shape

    @pl.when(pl.program_id(0) == 0)
    def _():
        first = f_ref[...]
        weights = w_ref[...].astype(jnp.float32)
        base = place[1] * cols

        def matrix(position):
            total = jnp.zeros(position.shape, jnp.float32)
            for k in range(4):
                tap = first + k
                tap = jnp.where(tap >= circle, tap - circle, tap)
                total = total + jnp.where(position == tap, weights[k : k + 1], 0.0)
            return total.astype(jnp.bfloat16)

        b_ref[...] = matrix(base + lax.broadcasted_iota(jnp.int32, (cols, out_cols), 0))
        row = lax.broadcasted_iota(jnp.int32, (16, out_cols), 0)
        low = base + row - 6
        low = jnp.where(low < 0, low + circle, low)
        high = base + cols + row - 8
        high = jnp.where(high >= circle, high - circle, high)
        position = jnp.where(
            jnp.logical_and(row >= 3, row < 6),
            low,
            jnp.where(jnp.logical_and(row >= 8, row < 11), high, -100),
        )
        e_ref[...] = matrix(position)

    @pl.loop(0, parents, unroll=2)
    def _(p):
        outside = jnp.concatenate([low_ref[p], high_ref[p]], axis=0)
        y = jnp.dot(h_ref[p], b_ref[...], preferred_element_type=jnp.float32)
        y = y + lax.dot_general(
            outside, e_ref[...], (((0,), (0,)), ((), ())), preferred_element_type=jnp.float32
        )
        both = apply_factors(y, chunk, [t_ref[k] for k in range(4)])
        for c in range(2):
            o_ref[p, c] = both[c]


def interpolate_phi(h, low, high, first, weights, factors, circle, place, rows, out_cols):
    parents, rows8, cols = h.shape
    group = math.gcd(parents, 4)
    edge_spec = pl.BlockSpec((group,) + low.shape[1:], lambda p, at: (p, 0, 0))

    def body(*refs):
        phi_kernel(circle, *refs)

    return pl.pallas_call(
        body,
        grid_spec=pltpu.PrefetchScalarGridSpec(
            num_scalar_prefetch=1,
            grid=(parents // group,),
            in_specs=[
                pl.BlockSpec((group, rows8, cols), lambda p, at: (p, 0, 0)),
                edge_spec,
                edge_spec,
                pl.BlockSpec((1, out_cols), lambda p, at: (0, at[1])),
                pl.BlockSpec((4, out_cols), lambda p, at: (0, at[1])),
                pl.BlockSpec((4, rows, out_cols), lambda p, at: (0, at[0], at[1])),
            ],
            out_specs=pl.BlockSpec((group, 2, rows, out_cols), lambda p, at: (p, 0, 0, 0)),
            scratch_shapes=[
                pltpu.VMEM((cols, out_cols), jnp.bfloat16),
                pltpu.VMEM((16, out_cols), jnp.bfloat16),
            ],
        ),
        out_shape=jax.ShapeDtypeStruct((parents, 2, rows, out_cols), jnp.bfloat16),
        compiler_params=pltpu.CompilerParams(vmem_limit_bytes=VMEM_LIMIT),
        cost_estimate=pl.CostEstimate(
            flops=2 * parents * rows8 * (cols + 16) * out_cols,
            bytes_accessed=4 * parents * rows8 * cols,
            transcendentals=0,
        ),
        name="level4",
    )(place, h, low, high, first, weights, factors)


def translate_kernel(slot_first, src, off, x_ref, t_ref, o_ref, held):
    targets = o_ref.shape[0]
    slots = src.shape[0 if slot_first else 1]
    parts, senders = x_ref.shape[:2]
    sources = parts * senders
    held[sources] = jnp.zeros(held.shape[1:], held.dtype)

    @pl.loop(0, senders)
    def _(s):
        for c in range(parts):
            held[s * parts + c] = x_ref[c, s]

    def read(ref, slot, t):
        return ref[slot, t] if slot_first else ref[t, slot]

    def gather(t, end):
        real = imag = None
        for first in range(0, end, 4):
            group_real = group_imag = None
            for j in range(first, min(first + 4, end)):
                picked = read(src, j, t)
                chosen = read(off, j, t)
                pr, pi = held[picked, 0], held[picked, 1]
                fr, fi = t_ref[chosen, 0], t_ref[chosen, 1]
                term_real = fr * pr - fi * pi
                term_imag = fr * pi + fi * pr
                group_real = term_real if group_real is None else group_real + term_real
                group_imag = term_imag if group_imag is None else group_imag + term_imag
            group_real = group_real.astype(jnp.float32)
            group_imag = group_imag.astype(jnp.float32)
            real = group_real if real is None else real + group_real
            imag = group_imag if imag is None else imag + group_imag
        o_ref[t, 0] = real.astype(o_ref.dtype)
        o_ref[t, 1] = imag.astype(o_ref.dtype)

    ends = [end for end in (8, 12) if end < slots] + [slots]

    @pl.loop(0, targets)
    def _(t):
        lower = 0
        for end in ends:
            wanted = read(src, lower, t) < sources
            if end < slots:
                wanted = jnp.logical_and(wanted, read(src, end, t) == sources)

            @pl.when(wanted)
            def _(end=end):
                gather(t, end)

            lower = end


def translate(patterns, table, sources, displacements, row_chunk, name):
    targets, slots = sources.shape
    displacement_count, _, rows, cols = table.shape
    parts, senders = patterns.shape[:2]
    src = jnp.where(sources < 0, parts * senders, sources)
    off = jnp.maximum(displacements, 0)
    slot_first = targets > slots
    if slot_first:
        src, off = src.T, off.T

    def body(*refs):
        translate_kernel(slot_first, *refs)

    return pl.pallas_call(
        body,
        grid_spec=pltpu.PrefetchScalarGridSpec(
            num_scalar_prefetch=2,
            grid=(rows // row_chunk,),
            in_specs=[
                pl.BlockSpec((parts, senders, 2, row_chunk, cols), lambda r, *_: (0, 0, 0, r, 0)),
                pl.BlockSpec((displacement_count, 2, row_chunk, cols), lambda r, *_: (0, 0, r, 0)),
            ],
            out_specs=pl.BlockSpec((targets, 2, row_chunk, cols), lambda r, *_: (0, 0, r, 0)),
            scratch_shapes=[pltpu.VMEM((parts * senders + 1, 2, row_chunk, cols), jnp.bfloat16)],
        ),
        out_shape=jax.ShapeDtypeStruct((targets, 2, rows, cols), jnp.bfloat16),
        compiler_params=pltpu.CompilerParams(vmem_limit_bytes=VMEM_LIMIT),
        cost_estimate=pl.CostEstimate(
            flops=8 * targets * slots * rows * cols,
            bytes_accessed=2 * (2 * targets * 2 * rows * cols + table.size),
            transcendentals=0,
        ),
        name=name,
    )(src, off, patterns, table)


def shards(
    patterns7,
    polar_up7,
    azimuth_up7,
    polar_up6,
    azimuth_up6,
    polar_first,
    polar_weights,
    azimuth_first,
    azimuth_weights,
    transfer5,
    sources5,
    offsets5,
    transfer4,
    sources4,
    offsets4,
):
    band_count = lax.axis_size("ang")
    block_count = lax.axis_size("clu")
    device_count = band_count * block_count
    band = lax.axis_index("ang")
    block = lax.axis_index("clu")
    rows_six, cols_six = polar_up7.shape[0], azimuth_up7.shape[1]
    rows_five, cols_five = polar_up6.shape[0], azimuth_up6.shape[1]
    rows_four, cols_four = polar_first.shape[0], azimuth_first.shape[0]
    source_rows, source_cols = rows_five // band_count, cols_five // block_count
    band_rows, block_cols = rows_four // band_count, cols_four // block_count

    parents6 = patterns7.shape[0] // 8
    parents5 = parents6 // 8
    assert parents5 == 4
    arrived5 = produce(
        patterns7,
        (
            polar_operator(polar_up7, (-1.0, 1.0), rows_six),
            polar_operator(polar_up6, (-1.0, 1.0), rows_five // 2),
        ),
        (azimuth_up7, azimuth_up6),
        (transverse_factors(rows_six, cols_six), transverse_factors(rows_five, cols_five)),
        block_count,
        band_count,
    )
    arrived5 = arrived5.reshape((parents5, device_count) + arrived5.shape[1:])

    upward = [(i, i + 1) for i in range(band_count - 1)]
    downward = [(i + 1, i) for i in range(band_count - 1)]
    low = lax.ppermute(arrived5[:, :, :, source_rows - 3 :], "ang", upward)
    high = lax.ppermute(arrived5[:, :, :, :3], "ang", downward)
    fill = jnp.zeros(arrived5.shape[:3] + (10, source_cols), jnp.bfloat16)
    edges5 = jnp.concatenate([low, high, fill], axis=3)

    axial = rows_four / 8.0 * np.cos(sample_angles(rows_four, 1)[0])
    stencil = jnp.concatenate(
        [
            polar_first.astype(jnp.float32)[:, None],
            polar_weights.astype(jnp.float32),
            jnp.asarray(np.stack([np.cos(axial), np.sin(axial), 0 * axial], 1), jnp.float32),
        ],
        axis=1,
    )
    place = jnp.stack([band, block]).astype(jnp.int32)
    picker = np.zeros((8, source_cols), np.float32)
    for k in range(3):
        picker[k, k] = 1.0
        picker[3 + k, source_cols - 3 + k] = 1.0
    shape4 = (parents5, device_count // 2, 2, 2)
    halfway4, edges4 = halfway(
        arrived5.reshape(shape4 + arrived5.shape[3:]),
        edges5.reshape(shape4 + edges5.shape[3:]),
        stencil,
        jnp.asarray(picker, jnp.bfloat16),
        place,
        band_rows,
    )
    around = [(i, (i + 1) % block_count) for i in range(block_count)]
    from_low = lax.ppermute(edges4, "clu", around)
    from_high = lax.ppermute(edges4, "clu", [(b, a) for a, b in around])
    translated5 = translate(
        arrived5, transfer5, sources5, offsets5, transfer5.shape[2], "translate5"
    )
    level4 = interpolate_phi(
        halfway4,
        from_low,
        from_high,
        azimuth_first[None],
        azimuth_weights.T,
        jnp.asarray(transverse_factors(rows_four, cols_four)),
        cols_five,
        place,
        band_rows,
        block_cols,
    )
    translated4 = translate(level4[None], transfer4, sources4, offsets4, 16, "translate4")
    return translated5, translated4


def solution(mesh):
    in_specs = (
        P(("clu", "ang"), None, None, None),
        P(),
        P(),
        P(),
        P(),
        P(),
        P(),
        P(),
        P(),
        P(None, None, "ang", "clu"),
        P(),
        P(),
        P(None, None, "ang", "clu"),
        P(),
        P(),
    )
    out_specs = (P(None, None, "ang", "clu"), P(None, None, "ang", "clu"))
    return jax.shard_map(shards, mesh=mesh, in_specs=in_specs, out_specs=out_specs, check_vma=False)
```

```python
import math

import jax
import jax.numpy as jnp
import numpy as np
from jax import lax
from jax.experimental import pallas as pl
from jax.experimental.pallas import tpu as pltpu
from jax.sharding import PartitionSpec as P

VMEM_LIMIT = 58 * 1024 * 1024


def sample_angles(rows, cols):
    polar = (np.arange(rows) + 0.5) * (np.pi / rows)
    azimuth = np.arange(cols) * (2.0 * np.pi / cols)
    return polar, azimuth


def transverse_factors(rows, cols):
    polar, azimuth = sample_angles(rows, cols)
    first = rows / 8.0 * np.sin(polar)[:, None] * np.cos(azimuth)[None, :]
    second = rows / 8.0 * np.sin(polar)[:, None] * np.sin(azimuth)[None, :]
    return np.stack(
        [
            np.cos(first) * np.cos(second),
            np.sin(first) * np.cos(second),
            np.cos(first) * np.sin(second),
            np.sin(first) * np.sin(second),
        ]
    ).astype(np.float32)


def polar_operator(matrix, signs, chunk):
    rows, taps = matrix.shape
    polar, _ = sample_angles(rows, 1)
    axial = rows / 8.0 * np.cos(polar)
    in_phase = matrix.astype(jnp.float32) * np.cos(axial).astype(np.float32)[:, None]
    quadrature = matrix.astype(jnp.float32) * np.sin(axial).astype(np.float32)[:, None]
    real_row = []
    imag_row = []
    for sign in signs:
        real_row += [in_phase, -sign * quadrature]
        imag_row += [sign * quadrature, in_phase]
    whole = jnp.stack([jnp.concatenate(real_row, axis=1), jnp.concatenate(imag_row, axis=1)])
    whole = whole.reshape(2, rows // chunk, chunk, 2 * len(signs) * taps)
    whole = whole.transpose(1, 0, 2, 3)
    return whole.reshape(rows // chunk, 2 * chunk, -1).astype(jnp.bfloat16)


def sign_sums(h, cols):
    h0, h1, h2, h3 = [h[:, k * cols : (k + 1) * cols] for k in range(4)]
    low_sum, low_diff = h0 + h1, h1 - h0
    high_sum, high_diff = h2 + h3, h3 - h2
    return jnp.concatenate(
        [
            (low_sum + high_sum).astype(jnp.bfloat16),
            (low_diff + high_diff).astype(jnp.bfloat16),
            (high_sum - low_sum).astype(jnp.bfloat16),
            (high_diff - low_diff).astype(jnp.bfloat16),
        ],
        axis=0,
    )


def apply_factors(y, chunk, factors):
    part = [y[k * chunk : (k + 1) * chunk] for k in range(8)]
    f0, f1, f2, f3 = factors
    real = f0 * part[0] - f1 * part[3] - f2 * part[5] - f3 * part[6]
    imag = f0 * part[1] + f1 * part[2] + f2 * part[4] - f3 * part[7]
    return real.astype(jnp.bfloat16), imag.astype(jnp.bfloat16)


def siblings(block, child, pairs):
    rows2, cols = block.shape[-3] * block.shape[-2], block.shape[-1]
    stacked = [block[4 * s + child].reshape(rows2, cols) for s in range(pairs)]
    return jnp.concatenate(stacked, axis=0)


def produce_kernel(
    clu, ang, x_ref, m6, b6, t6, m5, b5, t5, arrived, level6, windows, send_sem, recv_sem, own_sem
):
    step = pl.program_id(0)
    steps = pl.num_programs(0)
    devices = clu * ang
    me = lax.axis_index("clu") * ang + lax.axis_index("ang")

    @pl.when(step == 0)
    def _():
        barrier = pltpu.get_barrier_semaphore()

        @pl.loop(1, devices)
        def _(k):
            other = lax.rem(me + k, devices)
            pl.semaphore_signal(
                barrier,
                inc=1,
                device_id=(other // ang, lax.rem(other, ang)),
                device_id_type=pl.DeviceIdType.MESH,
            )

        pl.semaphore_wait(barrier, devices - 1)

    @pl.loop(0, 8, unroll=2)
    def _(p):
        cols = x_ref.shape[4]
        joined = jnp.concatenate([siblings(x_ref.at[p], o, 2) for o in range(4)], axis=1)
        h = jnp.dot(m6[...], joined, preferred_element_type=jnp.float32)
        sums = sign_sums(h, cols)
        y = jnp.dot(sums, b6[...], preferred_element_type=jnp.float32)
        both = apply_factors(y, t6.shape[1], [t6[k] for k in range(4)])
        for c in range(2):
            level6[p, c] = both[c]

    cols = level6.shape[3]
    chunks, chunk2 = m5.shape[:2]
    chunk = chunk2 // 2
    band_rows, block_cols = windows.shape[2], windows.shape[3]
    bands = chunk // band_rows
    width = min(256, b5.shape[1])

    @pl.loop(0, chunks)
    def _(u):
        joined = jnp.concatenate([siblings(level6, o, 2) for o in range(4)], axis=1)
        h = jnp.dot(m5[u], joined, preferred_element_type=jnp.float32)
        sums = sign_sums(h, cols)
        for j in range(b5.shape[1] // width):
            cut = slice(j * width, (j + 1) * width)
            y = jnp.dot(sums, b5[:, cut], preferred_element_type=jnp.float32)
            rows = pl.ds(pl.multiple_of(u * chunk, chunk), chunk)
            both = apply_factors(y, chunk, [t5[k, rows, cut] for k in range(4)])
            for c in range(2):
                for q in range(width // block_cols):
                    for band in range(bands):
                        target = (j * (width // block_cols) + q) * ang + u * bands + band
                        windows[step * devices + target, c] = both[c][
                            band * band_rows : (band + 1) * band_rows,
                            q * block_cols : (q + 1) * block_cols,
                        ]

    @pl.loop(1, devices)
    def _(k):
        other = lax.rem(me + k, devices)
        pltpu.make_async_remote_copy(
            src_ref=windows.at[step * devices + other],
            dst_ref=arrived.at[step * devices + me],
            send_sem=send_sem,
            recv_sem=recv_sem,
            device_id=(other // ang, lax.rem(other, ang)),
            device_id_type=pl.DeviceIdType.MESH,
        ).start()

    pltpu.make_async_copy(
        windows.at[step * devices + me], arrived.at[step * devices + me], own_sem.at[step]
    ).start()

    @pl.when(step == steps - 1)
    def _():
        away = pl.ds(0, 4 * (devices - 1))
        everything = pltpu.make_async_remote_copy(
            src_ref=windows.at[away],
            dst_ref=arrived.at[away],
            send_sem=send_sem,
            recv_sem=recv_sem,
            device_id=(lax.axis_index("clu"), lax.rem(lax.axis_index("ang") + 1, ang)),
            device_id_type=pl.DeviceIdType.MESH,
        )
        everything.wait_send()
        everything.wait_recv()
        for k in range(4):
            pltpu.make_async_copy(
                windows.at[k * devices + me], arrived.at[k * devices + me], own_sem.at[k]
            ).wait()


def produce(children, operators, azimuths, factors, clu, ang):
    parents = children.shape[0] // 64
    rows, cols = factors[1].shape[1:]
    window = (2, rows // ang, cols // clu)
    devices = clu * ang

    def body(*refs):
        produce_kernel(clu, ang, *refs)

    def whole(array):
        zeros = (0,) * array.ndim
        return pl.BlockSpec(array.shape, lambda p: zeros)

    arguments = [operators[0][0], azimuths[0], factors[0], operators[1], azimuths[1], factors[1]]
    return pl.pallas_call(
        body,
        grid=(parents,),
        in_specs=[pl.BlockSpec((8, 8) + children.shape[1:], lambda p: (p, 0, 0, 0, 0))]
        + [whole(array) for array in arguments],
        out_specs=pl.BlockSpec(memory_space=pl.ANY),
        out_shape=jax.ShapeDtypeStruct((parents * devices,) + window, jnp.bfloat16),
        scratch_shapes=[
            pltpu.VMEM((8, 2) + factors[0].shape[1:], jnp.bfloat16),
            pltpu.VMEM((parents * devices,) + window, jnp.bfloat16),
            pltpu.SemaphoreType.DMA,
            pltpu.SemaphoreType.DMA,
            pltpu.SemaphoreType.DMA((4,)),
        ],
        compiler_params=pltpu.CompilerParams(
            vmem_limit_bytes=VMEM_LIMIT, collective_id=0, has_side_effects=True
        ),
        name="produce",
    )(children.reshape((-1, 8) + children.shape[1:]), *arguments)


def halfway_kernel(place, s_ref, e_ref, x_ref, edge_ref, h_ref, g_ref, m_ref):
    _, parents, _, _, rows, cols = x_ref.shape
    edge_rows = edge_ref.shape[4]
    band_rows = s_ref.shape[0]

    @pl.when(pl.program_id(0) == 0)
    def _():
        stencil = s_ref[...]
        first = stencil[:, 0:1].astype(jnp.int32) - place[0] * rows

        def matrix(position):
            total = jnp.zeros(position.shape, jnp.float32)
            for k in range(4):
                total = total + jnp.where(position == first + k, stencil[:, 1 + k : 2 + k], 0.0)
            return total

        inner = lax.broadcasted_iota(jnp.int32, (band_rows, rows), 1)
        outer = lax.broadcasted_iota(jnp.int32, (band_rows, edge_rows), 1)
        outer = jnp.where(outer < 3, outer - 3, jnp.where(outer < 6, outer + rows - 3, -100))
        start = 0
        for whole in (matrix(inner), matrix(outer)):
            in_phase = (whole * stencil[:, 5:6]).astype(jnp.bfloat16)
            quadrature = (whole * stencil[:, 6:7]).astype(jnp.bfloat16)
            width = whole.shape[1]
            for left, right in ((in_phase, quadrature), (in_phase, -quadrature)):
                m_ref[:band_rows, start : start + width] = left
                m_ref[band_rows:, start : start + width] = -right
                m_ref[:band_rows, start + width : start + 2 * width] = right
                m_ref[band_rows:, start + width : start + 2 * width] = left
                start += 2 * width

    @pl.loop(0, parents, unroll=2)
    def _(p):
        family = []
        for o in range(4):
            pieces = [x_ref[o, p, s].reshape(2 * rows, cols) for s in range(2)]
            pieces += [edge_ref[o, p, s].reshape(2 * edge_rows, cols) for s in range(2)]
            family.append(jnp.concatenate(pieces, axis=0))
        joined = jnp.concatenate(family, axis=1)
        h = jnp.dot(m_ref[...], joined, preferred_element_type=jnp.float32)
        sums = sign_sums(h, cols)
        h_ref[p] = sums
        edges = lax.dot_general(
            e_ref[...], sums, (((1,), (1,)), ((), ())), preferred_element_type=jnp.float32
        )
        g_ref[p] = edges.astype(jnp.bfloat16)


def halfway(main, edges, stencil, picker, place, band_rows):
    _, parents, _, _, rows, cols = main.shape
    edge_rows = edges.shape[4]
    group = math.gcd(parents, 4)
    out_rows = 8 * band_rows
    depth = 4 * (rows + edge_rows)
    return pl.pallas_call(
        halfway_kernel,
        grid_spec=pltpu.PrefetchScalarGridSpec(
            num_scalar_prefetch=1,
            grid=(parents // group,),
            in_specs=[
                pl.BlockSpec((band_rows, stencil.shape[1]), lambda p, at: (at[0], 0)),
                pl.BlockSpec(picker.shape, lambda p, at: (0, 0)),
                pl.BlockSpec((4, group, 2, 2, rows, cols), lambda p, at: (0, p, 0, 0, 0, 0)),
                pl.BlockSpec((4, group, 2, 2, edge_rows, cols), lambda p, at: (0, p, 0, 0, 0, 0)),
            ],
            out_specs=[
                pl.BlockSpec((group, out_rows, cols), lambda p, at: (p, 0, 0)),
                pl.BlockSpec((group, picker.shape[0], out_rows), lambda p, at: (p, 0, 0)),
            ],
            scratch_shapes=[pltpu.VMEM((2 * band_rows, depth), jnp.bfloat16)],
        ),
        out_shape=[
            jax.ShapeDtypeStruct((parents, out_rows, cols), jnp.bfloat16),
            jax.ShapeDtypeStruct((parents, picker.shape[0], out_rows), jnp.bfloat16),
        ],
        compiler_params=pltpu.CompilerParams(vmem_limit_bytes=VMEM_LIMIT),
        cost_estimate=pl.CostEstimate(
            flops=2 * parents * out_rows * depth * cols,
            bytes_accessed=4 * parents * out_rows * cols,
            transcendentals=0,
        ),
        name="halfway4",
    )(place, stencil, picker, main, edges)


def phi_kernel(circle, place, h_ref, low_ref, high_ref, f_ref, w_ref, t_ref, o_ref, b_ref, e_ref):
    parents = h_ref.shape[0]
    chunk = t_ref.shape[1]
    cols, out_cols = b_ref.shape

    @pl.when(pl.program_id(0) == 0)
    def _():
        first = f_ref[...]
        weights = w_ref[...].astype(jnp.float32)
        base = place[1] * cols

        def matrix(position):
            total = jnp.zeros(position.shape, jnp.float32)
            for k in range(4):
                tap = first + k
                tap = jnp.where(tap >= circle, tap - circle, tap)
                total = total + jnp.where(position == tap, weights[k : k + 1], 0.0)
            return total.astype(jnp.bfloat16)

        b_ref[...] = matrix(base + lax.broadcasted_iota(jnp.int32, (cols, out_cols), 0))
        row = lax.broadcasted_iota(jnp.int32, (16, out_cols), 0)
        low = base + row - 6
        low = jnp.where(low < 0, low + circle, low)
        high = base + cols + row - 8
        high = jnp.where(high >= circle, high - circle, high)
        position = jnp.where(
            jnp.logical_and(row >= 3, row < 6),
            low,
            jnp.where(jnp.logical_and(row >= 8, row < 11), high, -100),
        )
        e_ref[...] = matrix(position)

    @pl.loop(0, parents, unroll=2)
    def _(p):
        outside = jnp.concatenate([low_ref[p], high_ref[p]], axis=0)
        y = jnp.dot(h_ref[p], b_ref[...], preferred_element_type=jnp.float32)
        y = y + lax.dot_general(
            outside, e_ref[...], (((0,), (0,)), ((), ())), preferred_element_type=jnp.float32
        )
        both = apply_factors(y, chunk, [t_ref[k] for k in range(4)])
        for c in range(2):
            o_ref[p, c] = both[c]


def interpolate_phi(h, low, high, first, weights, factors, circle, place, rows, out_cols):
    parents, rows8, cols = h.shape
    group = math.gcd(parents, 4)
    edge_spec = pl.BlockSpec((group,) + low.shape[1:], lambda p, at: (p, 0, 0))

    def body(*refs):
        phi_kernel(circle, *refs)

    return pl.pallas_call(
        body,
        grid_spec=pltpu.PrefetchScalarGridSpec(
            num_scalar_prefetch=1,
            grid=(parents // group,),
            in_specs=[
                pl.BlockSpec((group, rows8, cols), lambda p, at: (p, 0, 0)),
                edge_spec,
                edge_spec,
                pl.BlockSpec((1, out_cols), lambda p, at: (0, at[1])),
                pl.BlockSpec((4, out_cols), lambda p, at: (0, at[1])),
                pl.BlockSpec((4, rows, out_cols), lambda p, at: (0, at[0], at[1])),
            ],
            out_specs=pl.BlockSpec((group, 2, rows, out_cols), lambda p, at: (p, 0, 0, 0)),
            scratch_shapes=[
                pltpu.VMEM((cols, out_cols), jnp.bfloat16),
                pltpu.VMEM((16, out_cols), jnp.bfloat16),
            ],
        ),
        out_shape=jax.ShapeDtypeStruct((parents, 2, rows, out_cols), jnp.bfloat16),
        compiler_params=pltpu.CompilerParams(vmem_limit_bytes=VMEM_LIMIT),
        cost_estimate=pl.CostEstimate(
            flops=2 * parents * rows8 * (cols + 16) * out_cols,
            bytes_accessed=4 * parents * rows8 * cols,
            transcendentals=0,
        ),
        name="level4",
    )(place, h, low, high, first, weights, factors)


def translate_kernel(slot_first, src, off, x_ref, t_ref, o_ref, held):
    targets = o_ref.shape[0]
    slots = src.shape[0 if slot_first else 1]
    parts, senders = x_ref.shape[:2]
    sources = parts * senders
    held[sources] = jnp.zeros(held.shape[1:], held.dtype)

    @pl.loop(0, senders)
    def _(s):
        for c in range(parts):
            held[s * parts + c] = x_ref[c, s]

    def read(ref, slot, t):
        return ref[slot, t] if slot_first else ref[t, slot]

    def gather(t, end):
        real = imag = None
        for first in range(0, end, 4):
            group_real = group_imag = None
            for j in range(first, min(first + 4, end)):
                picked = read(src, j, t)
                chosen = read(off, j, t)
                pr, pi = held[picked, 0], held[picked, 1]
                fr, fi = t_ref[chosen, 0], t_ref[chosen, 1]
                term_real = fr * pr - fi * pi
                term_imag = fr * pi + fi * pr
                group_real = term_real if group_real is None else group_real + term_real
                group_imag = term_imag if group_imag is None else group_imag + term_imag
            group_real = group_real.astype(jnp.float32)
            group_imag = group_imag.astype(jnp.float32)
            real = group_real if real is None else real + group_real
            imag = group_imag if imag is None else imag + group_imag
        o_ref[t, 0] = real.astype(o_ref.dtype)
        o_ref[t, 1] = imag.astype(o_ref.dtype)

    ends = [end for end in (8, 12) if end < slots] + [slots]

    @pl.loop(0, targets)
    def _(t):
        lower = 0
        for end in ends:
            wanted = read(src, lower, t) < sources
            if end < slots:
                wanted = jnp.logical_and(wanted, read(src, end, t) == sources)

            @pl.when(wanted)
            def _(end=end):
                gather(t, end)

            lower = end


def translate(patterns, table, sources, displacements, row_chunk, name):
    targets, slots = sources.shape
    displacement_count, _, rows, cols = table.shape
    parts, senders = patterns.shape[:2]
    src = jnp.where(sources < 0, parts * senders, sources)
    off = jnp.maximum(displacements, 0)
    slot_first = targets > slots
    if slot_first:
        src, off = src.T, off.T

    def body(*refs):
        translate_kernel(slot_first, *refs)

    return pl.pallas_call(
        body,
        grid_spec=pltpu.PrefetchScalarGridSpec(
            num_scalar_prefetch=2,
            grid=(rows // row_chunk,),
            in_specs=[
                pl.BlockSpec((parts, senders, 2, row_chunk, cols), lambda r, *_: (0, 0, 0, r, 0)),
                pl.BlockSpec((displacement_count, 2, row_chunk, cols), lambda r, *_: (0, 0, r, 0)),
            ],
            out_specs=pl.BlockSpec((targets, 2, row_chunk, cols), lambda r, *_: (0, 0, r, 0)),
            scratch_shapes=[pltpu.VMEM((parts * senders + 1, 2, row_chunk, cols), jnp.bfloat16)],
        ),
        out_shape=jax.ShapeDtypeStruct((targets, 2, rows, cols), jnp.bfloat16),
        compiler_params=pltpu.CompilerParams(vmem_limit_bytes=VMEM_LIMIT),
        cost_estimate=pl.CostEstimate(
            flops=8 * targets * slots * rows * cols,
            bytes_accessed=2 * (2 * targets * 2 * rows * cols + table.size),
            transcendentals=0,
        ),
        name=name,
    )(src, off, patterns, table)


def shards(
    patterns7,
    polar_up7,
    azimuth_up7,
    polar_up6,
    azimuth_up6,
    polar_first,
    polar_weights,
    azimuth_first,
    azimuth_weights,
    transfer5,
    sources5,
    offsets5,
    transfer4,
    sources4,
    offsets4,
):
    band_count = lax.axis_size("ang")
    block_count = lax.axis_size("clu")
    device_count = band_count * block_count
    band = lax.axis_index("ang")
    block = lax.axis_index("clu")
    rows_six, cols_six = polar_up7.shape[0], azimuth_up7.shape[1]
    rows_five, cols_five = polar_up6.shape[0], azimuth_up6.shape[1]
    rows_four, cols_four = polar_first.shape[0], azimuth_first.shape[0]
    source_rows, source_cols = rows_five // band_count, cols_five // block_count
    band_rows, block_cols = rows_four // band_count, cols_four // block_count

    parents6 = patterns7.shape[0] // 8
    parents5 = parents6 // 8
    assert parents5 == 4
    arrived5 = produce(
        patterns7,
        (
            polar_operator(polar_up7, (-1.0, 1.0), rows_six),
            polar_operator(polar_up6, (-1.0, 1.0), rows_five // 2),
        ),
        (azimuth_up7, azimuth_up6),
        (transverse_factors(rows_six, cols_six), transverse_factors(rows_five, cols_five)),
        block_count,
        band_count,
    )
    arrived5 = arrived5.reshape((parents5, device_count) + arrived5.shape[1:])

    upward = [(i, i + 1) for i in range(band_count - 1)]
    downward = [(i + 1, i) for i in range(band_count - 1)]
    low = lax.ppermute(arrived5[:, :, :, source_rows - 3 :], "ang", upward)
    high = lax.ppermute(arrived5[:, :, :, :3], "ang", downward)
    fill = jnp.zeros(arrived5.shape[:3] + (10, source_cols), jnp.bfloat16)
    edges5 = jnp.concatenate([low, high, fill], axis=3)

    axial = rows_four / 8.0 * np.cos(sample_angles(rows_four, 1)[0])
    stencil = jnp.concatenate(
        [
            polar_first.astype(jnp.float32)[:, None],
            polar_weights.astype(jnp.float32),
            jnp.asarray(np.stack([np.cos(axial), np.sin(axial), 0 * axial], 1), jnp.float32),
        ],
        axis=1,
    )
    place = jnp.stack([band, block]).astype(jnp.int32)
    picker = np.zeros((8, source_cols), np.float32)
    for k in range(3):
        picker[k, k] = 1.0
        picker[3 + k, source_cols - 3 + k] = 1.0
    shape4 = (parents5, device_count // 2, 2, 2)
    halfway4, edges4 = halfway(
        arrived5.reshape(shape4 + arrived5.shape[3:]),
        edges5.reshape(shape4 + edges5.shape[3:]),
        stencil,
        jnp.asarray(picker, jnp.bfloat16),
        place,
        band_rows,
    )
    edges4, sources5 = lax.optimization_barrier((edges4, sources5))
    around = [(i, (i + 1) % block_count) for i in range(block_count)]
    from_low = lax.ppermute(edges4, "clu", around)
    from_high = lax.ppermute(edges4, "clu", [(b, a) for a, b in around])
    translated5 = translate(
        arrived5, transfer5, sources5, offsets5, transfer5.shape[2], "translate5"
    )
    level4 = interpolate_phi(
        halfway4,
        from_low,
        from_high,
        azimuth_first[None],
        azimuth_weights.T,
        jnp.asarray(transverse_factors(rows_four, cols_four)),
        cols_five,
        place,
        band_rows,
        block_cols,
    )
    translated4 = translate(level4[None], transfer4, sources4, offsets4, 16, "translate4")
    return translated5, translated4


def solution(mesh):
    in_specs = (
        P(("clu", "ang"), None, None, None),
        P(),
        P(),
        P(),
        P(),
        P(),
        P(),
        P(),
        P(),
        P(None, None, "ang", "clu"),
        P(),
        P(),
        P(None, None, "ang", "clu"),
        P(),
        P(),
    )
    out_specs = (P(None, None, "ang", "clu"), P(None, None, "ang", "clu"))
    return jax.shard_map(shards, mesh=mesh, in_specs=in_specs, out_specs=out_specs, check_vma=False)
```
